32 devices in a mesh: groups: 2 (over x), col: 8 (over z, y), row: 2 (over core).
Axes of the slice: x: 2, y: 2, z: 4, core: 2. Of those that a mesh axis runs over, the one named last changes fastest.
Arguments:
- queries: bfloat16 [32, 8, 64, 1536], P(('groups', 'row'), 'col'), parts along dimension 0, may hold values from -300 to 300
- key_mant: bfloat16 [32, 8, 64, 1536], P(('groups', 'row'), 'col'), parts along dimension 0, may hold values from -8 to 8
- key_exp: int32 [32, 8, 2, 1536], P(('groups', 'row'), 'col'), parts along dimension 0, may hold values from -1 to 1
- value_mant: bfloat16 [32, 8, 64, 1536], P(('groups', 'row'), 'col'), parts along dimension 0, may hold values from -4 to 4
- value_exp: int32 [32, 8, 2, 1536], P(('groups', 'row'), 'col'), parts along dimension 0, may hold values from 0 to 2
- cycle_list: int32 [4, 8, 4], P(('groups', 'row'), 'col'), parts along dimension 0, may hold values from 0 to 17, as said below
- dilated_list: int32 [4, 8, 4], P(('groups', 'row'), 'col'), parts along dimension 0, may hold values from 0 to 13, as said below
Outputs:
- attended: bfloat16 [32, 8, 64, 1536], P(('groups', 'row'), 'col'), parts along dimension 0
The draws below stay inside these ranges and needn't reach their ends.
There are 2 independent parts, one for each index of `groups`. The reference program is written for one: setup_inputs(seed, part) draws one part's arguments, and reference() takes and returns one part's arrays. A program takes and returns all parts, laid end to end along the dimension named above; each array names one. Nothing has to cross between parts.
Inputs may be any that keep to these rules, and one draw needn't show every extreme that they name: `cycle_list`: the 4 entries of a tile are distinct; none names a block outside the image, and every side of the cycle that lies inside the image is named at least once. `dilated_list`: the 4 entries of a tile are distinct.
All inputs are finite; a program needn't handle non-finite values.
Results may differ from the reference program's by a relative error of at most 0.0043.
Values may be sent and summed in bfloat16 or wider, within the bound.
A program may use at most 128 MiB of HBM per device.

```python
import jax
import jax.numpy as jnp
from jax import lax

HEADS = 12
HEAD_DIM = 128
DA = 1536
BLOCK = 64
QG = 32
TILE_BLOCK_ROWS = 8
DILATION_TILES = 8
TILE_ROWS = 2
IMAGE_TILE_COLS = 8
GR = 16
GC = 8
NB = 4
ND = 4


def key_field(key):
    normal_part = jnp.clip(jax.random.normal(jax.random.fold_in(key, 11), (GR, GC, BLOCK, DA), jnp.float32), -4.0, 4.0)
    return normal_part


def draw_key_mant(key, part):
    return key_field(key).astype(jnp.bfloat16)


def draw_queries(key, part):
    drawn = jnp.clip(jax.random.normal(jax.random.fold_in(key, 31), (GR, GC, BLOCK, DA), jnp.float32), -4.0, 4.0)
    return drawn.astype(jnp.bfloat16)


def draw_cycle_list(key, part):
    cycle_count = 2 * TILE_BLOCK_ROWS + 2
    candidate = jnp.arange(cycle_count, dtype=jnp.int32)[None, None, :]
    cycle_side = jnp.where(candidate == 0, 0, jnp.where(candidate == 1, 1, jnp.where(candidate < TILE_BLOCK_ROWS + 2, 2, 3)))
    cycle_place = jnp.where(candidate < 2, 0, jnp.where(candidate < TILE_BLOCK_ROWS + 2, candidate - 2, candidate - 2 - TILE_BLOCK_ROWS))
    tile_row = jnp.arange(TILE_ROWS, dtype=jnp.int32)[:, None, None]
    tile_col = jnp.arange(IMAGE_TILE_COLS, dtype=jnp.int32)[None, :, None]
    inside = (cycle_side == 0) & (tile_row > 0) | (cycle_side == 1) & (tile_row < TILE_ROWS - 1) | (cycle_side == 2) & (tile_col > 0) | (cycle_side == 3) & (tile_col < IMAGE_TILE_COLS - 1)
    picked = jax.random.randint(jax.random.fold_in(key, 41), (TILE_ROWS, IMAGE_TILE_COLS, 2), 0, TILE_BLOCK_ROWS)
    forced = (cycle_side < 2) | (cycle_side == 2) & (cycle_place == picked[:, :, 0:1]) | (cycle_side == 3) & (cycle_place == picked[:, :, 1:2])
    jitter = jax.random.randint(jax.random.fold_in(key, 42), (TILE_ROWS, IMAGE_TILE_COLS, cycle_count), 0, 1 << 20)
    ranking = jitter * cycle_count + candidate + forced.astype(jnp.int32) * (1 << 28)
    ranking = jnp.where(inside, ranking, -1 - candidate)
    return lax.top_k(ranking, NB)[1].astype(jnp.int32)


def draw_dilated_list(key, part):
    distant_count = (DILATION_TILES - 1) * (TILE_BLOCK_ROWS // 4)
    candidate = jnp.arange(distant_count, dtype=jnp.int32)[None, None, :]
    jitter = jax.random.randint(jax.random.fold_in(key, 51), (TILE_ROWS, IMAGE_TILE_COLS, distant_count), 0, 1 << 20)
    ranking = jitter * distant_count + candidate
    return lax.top_k(ranking, ND)[1].astype(jnp.int32)


def plant(drawn, stream_key, smallest, high):
    spot = [jax.random.randint(jax.random.fold_in(stream_key, axis), (), 0, length) for axis, length in enumerate(drawn.shape)]
    main_axis = drawn.shape.index(max(drawn.shape))
    beside = spot[:main_axis] + [(spot[main_axis] + 1) % drawn.shape[main_axis]] + spot[main_axis + 1:]
    return drawn.at[tuple(spot)].set(smallest).at[tuple(beside)].set(high)


def block_levels(key, shape, split, least, top_value):
    loudness = 1.0
    for axis_at, shards_of in split:
        draws = jax.random.uniform(jax.random.fold_in(jax.random.fold_in(key, 6), axis_at), (shards_of,), jnp.float32, least / len(split), top_value / len(split))
        loudness = loudness * jnp.repeat(jnp.exp(draws), shape[axis_at] // shards_of).reshape((-1,) + (1,) * (len(shape) - 1 - axis_at))
    return loudness


def gaussian(own_key, extent, spread, most, cuts=(), kind=jnp.bfloat16):
    loudness = block_levels(own_key, extent, cuts, -0.22, 0.18) if cuts else 1.0
    values = jax.random.normal(own_key, extent, jnp.float32) * spread * loudness
    return jnp.minimum(jnp.maximum(values, -most), most).astype(kind)


def setup_inputs(seed: int = 0, part: int = 0) -> dict:
    splits = jax.random.split(jax.random.key(seed), 8)
    own_keys = jax.random.split(jax.random.fold_in(splits[7], part), 8)
    queries = draw_queries(jax.random.fold_in(jax.random.fold_in(splits[7], part), 71), part)
    key_mant = draw_key_mant(jax.random.fold_in(jax.random.fold_in(splits[7], part), 71), part)
    key_exp = plant(jax.random.randint(own_keys[2], (GR, GC, BLOCK // QG, DA), -1, 2), jax.random.fold_in(own_keys[2], 1), -1, 1).astype(jnp.int32)
    value_mant = gaussian(own_keys[3], (GR, GC, BLOCK, DA), 1.0, 4.0, ((0, 2), (1, 8)))
    value_exp = plant(jax.random.randint(own_keys[4], (GR, GC, BLOCK // QG, DA), 0, 3), jax.random.fold_in(own_keys[4], 1), 0, 2).astype(jnp.int32)
    cycle_list = draw_cycle_list(jax.random.fold_in(jax.random.fold_in(splits[7], part), 71), part)
    dilated_list = draw_dilated_list(jax.random.fold_in(jax.random.fold_in(splits[7], part), 71), part)
    return dict(queries=queries, key_mant=key_mant, key_exp=key_exp, value_mant=value_mant, value_exp=value_exp, cycle_list=cycle_list, dilated_list=dilated_list)


def dequant(mantissa, exponent):
    factor = jnp.exp2(jnp.repeat(exponent, QG, axis=2).astype(jnp.float32))
    return (mantissa.astype(jnp.float32) * factor).astype(jnp.bfloat16)


def attend(query_tile, key_tile, value_tile):
    query_heads = query_tile.astype(jnp.float32).reshape(-1, HEADS, HEAD_DIM)
    key_heads = key_tile.astype(jnp.float32).reshape(-1, HEADS, HEAD_DIM)
    value_heads = value_tile.astype(jnp.float32).reshape(-1, HEADS, HEAD_DIM)
    scores = jnp.einsum("qhd,khd->hqk", query_heads, key_heads) * (HEAD_DIM ** -0.5)
    row_max = jnp.max(scores, axis=-1, keepdims=True)
    weights = jnp.exp(scores - row_max)
    row_total = jnp.sum(weights, axis=-1)
    rounded = lax.optimization_barrier(weights.astype(jnp.bfloat16))
    blended = jnp.einsum("hqk,khd->qhd", rounded.astype(jnp.float32), value_heads)
    return (blended / jnp.transpose(row_total)[:, :, None]).astype(jnp.bfloat16).reshape(-1, DA)


def reference(queries, key_mant, key_exp, value_mant, value_exp, cycle_list, dilated_list):
    stacked = jnp.stack([dequant(key_mant, key_exp), dequant(value_mant, value_exp)])
    step_spacing = IMAGE_TILE_COLS // DILATION_TILES
    distant_rows = TILE_BLOCK_ROWS // 4

    def one_tile(tile_index):
        tile_row = tile_index // IMAGE_TILE_COLS
        tile_col = (tile_index % IMAGE_TILE_COLS).astype(jnp.int32)
        first_row = (tile_row * TILE_BLOCK_ROWS).astype(jnp.int32)
        zero_index = jnp.zeros((), jnp.int32)
        query_tile = lax.dynamic_slice(queries, (first_row, tile_col, zero_index, zero_index), (TILE_BLOCK_ROWS, 1, BLOCK, DA)).reshape(TILE_BLOCK_ROWS * BLOCK, DA)
        own_blocks = lax.dynamic_slice(stacked, (zero_index, first_row, tile_col, zero_index, zero_index), (2, TILE_BLOCK_ROWS, 1, BLOCK, DA)).reshape(2, TILE_BLOCK_ROWS, BLOCK, DA)
        cycle_entry = cycle_list[tile_row, tile_col]
        cycle_row = jnp.where(cycle_entry == 0, -1, jnp.where(cycle_entry == 1, TILE_BLOCK_ROWS, jnp.where(cycle_entry < TILE_BLOCK_ROWS + 2, cycle_entry - 2, cycle_entry - 2 - TILE_BLOCK_ROWS)))
        cycle_col = jnp.where(cycle_entry < 2, 0, jnp.where(cycle_entry < TILE_BLOCK_ROWS + 2, -1, 1))
        source_row = jnp.clip(first_row + cycle_row, 0, GR - 1).astype(jnp.int32)
        source_col = jnp.clip(tile_col + cycle_col, 0, GC - 1).astype(jnp.int32)
        cycle_blocks = stacked[:, source_row, source_col]
        dilated_entry = dilated_list[tile_row, tile_col]
        hop_count = dilated_entry // distant_rows + 1
        row_place = dilated_entry % distant_rows
        far_col = ((tile_col + hop_count * step_spacing) % IMAGE_TILE_COLS).astype(jnp.int32)
        far_row = (first_row + 4 * row_place).astype(jnp.int32)
        dilated_blocks = stacked[:, far_row, far_col]
        key_values = jnp.concatenate([own_blocks, cycle_blocks, dilated_blocks], axis=1).reshape(2, -1, DA)
        return attend(query_tile, key_values[0], key_values[1])

    tiles = lax.map(one_tile, jnp.arange(TILE_ROWS * IMAGE_TILE_COLS, dtype=jnp.int32))
    return tiles.reshape(TILE_ROWS, IMAGE_TILE_COLS, TILE_BLOCK_ROWS, BLOCK, DA).transpose(0, 2, 1, 3, 4).reshape(GR, GC, BLOCK, DA)
```

```python
import functools
import math

import jax
import jax.numpy as jnp
from jax import lax
from jax.experimental import pallas as pl
from jax.experimental.pallas import tpu as pltpu
from jax.sharding import PartitionSpec as P

HEADS = 12
HEAD_DIM = 128
DILATION_TILES = 8
LINE = DILATION_TILES // 2
CHUNKS = 4
QUERY_TILE = 256
SLOTS = 3
MESH = pl.DeviceIdType.MESH


def request_tables(cycle_entry, dilated_entry, tile_blocks, member):
    is_left = (cycle_entry >= 2) & (cycle_entry < tile_blocks + 2)
    is_right = cycle_entry >= tile_blocks + 2

    def ranked(mask):
        before = jnp.arange(mask.shape[0])[:, None] > jnp.arange(mask.shape[0])[None, :]
        return jnp.sum((before & mask[None, :]).astype(jnp.int32), axis=1)

    def wanted(mask, rank, rows):
        slots = jnp.arange(SLOTS)[:, None]
        hit = mask[None, :] & (rank[None, :] == slots)
        return jnp.sum(jnp.where(hit, rows[None, :], 0), axis=1)

    left_rank, right_rank = ranked(is_left), ranked(is_right)
    left_rows = wanted(is_left, left_rank, cycle_entry - 2)
    right_rows = wanted(is_right, right_rank, cycle_entry - 2 - tile_blocks)
    cycle_slot = jnp.where(
        is_left, left_rank, jnp.where(is_right, SLOTS + right_rank, 2 * SLOTS)
    )
    distant_rows = tile_blocks // 4
    hop = dilated_entry // distant_rows + 1
    source = lax.rem(member + hop, DILATION_TILES)
    line_slot = (source // 2) * distant_rows + lax.rem(dilated_entry, distant_rows)
    crossing = lax.rem(hop, 2)
    asked = jnp.concatenate([line_slot * crossing, left_rows, right_rows]).astype(jnp.int32)
    asked = jnp.pad(asked[None, :], ((0, 7), (0, 128 - asked.shape[0])))
    places = jnp.concatenate([cycle_slot, line_slot * (1 - crossing), crossing])
    return asked, places.astype(jnp.int32)


def kernel(cols, blocks, places, q_ref, km_ref, ke_ref, vm_ref, ve_ref, asked, out_ref, *scratch):
    kv = scratch[0:CHUNKS]
    zbuf = scratch[CHUNKS : 2 * CHUNKS]
    pbuf = scratch[2 * CHUNKS : 3 * CHUNKS]
    cbuf = scratch[3 * CHUNKS : 4 * CHUNKS]
    psend = scratch[4 * CHUNKS : 5 * CHUNKS]
    csend = scratch[5 * CHUNKS : 6 * CHUNKS]
    (heard, heard_s, req_send, req_recv, req_local, z_send, z_recv, f_send, p_send, p_recv,
     c_send, c_recv, e_send, e_recv, v_send, v_recv) = scratch[6 * CHUNKS :]
    width = kv[0].shape[-1]
    block = kv[0].shape[-2]
    groups = ke_ref.shape[1]
    distant = blocks // 4
    spacing = cols // DILATION_TILES

    col = lax.axis_index("col")
    row = lax.axis_index("row")
    member, offset = col // spacing, lax.rem(col, spacing)
    gz, gy = member // 2, lax.rem(member, 2)

    def on_line(z):
        return {"col": (z * 2 + gy) * spacing + offset}

    partner = {"col": (gz * 2 + 1 - gy) * spacing + offset}
    left, right = {"col": col - 1}, {"col": col + 1}
    other = {"row": 1 - row}
    has_left, has_right = col > 0, col < cols - 1

    barrier = pltpu.get_barrier_semaphore()

    def greet(device):
        pl.semaphore_signal(barrier, inc=1, device_id=device, device_id_type=MESH)

    for z in range(LINE):
        pl.when(gz != z)(functools.partial(greet, on_line(z)))
    greet(partner)
    greet(other)
    pl.when(has_left)(functools.partial(greet, left))
    pl.when(has_right)(functools.partial(greet, right))

    def dequant(b):
        for which, (mant, expo) in enumerate(((km_ref, ke_ref), (vm_ref, ve_ref))):
            factor = lax.shift_left(jnp.int32(1), expo[b] + 8).astype(jnp.float32) * (2.0**-8)
            size = block // groups
            parts = [
                mant[b, g * size : (g + 1) * size, :].astype(jnp.float32) * factor[g : g + 1, :]
                for g in range(groups)
            ]
            full = jnp.concatenate(parts, axis=0).astype(jnp.bfloat16)
            for c in range(CHUNKS):
                kv[c][b, which] = full[:, c * width : (c + 1) * width]

    for r in range(distant):
        dequant(4 * r)
        for c in range(CHUNKS):
            zbuf[c][gz * distant + r] = kv[c][4 * r]

    pl.semaphore_wait(barrier, LINE + 1 + has_left.astype(jnp.int32) + has_right.astype(jnp.int32))

    def copy(src, dst, send, recv, device):
        return pltpu.make_async_remote_copy(
            src_ref=src, dst_ref=dst, send_sem=send, recv_sem=recv,
            device_id=device, device_id_type=MESH,
        )

    def ask(k, device):
        return copy(asked, heard.at[k], req_send.at[k], req_recv.at[k], device)

    ask(0, partner).start()
    pl.when(has_left)(lambda: ask(2, left).start())
    pl.when(has_right)(lambda: ask(1, right).start())

    def line_copy(c, source, z, sem):
        part = zbuf[c].at[pl.ds(source * distant, distant)]
        return copy(part, part, sem, z_recv.at[c, source], on_line(z))

    steps = (1, -1, 2, -2)

    def reaches(step):
        return (gz + step >= 0) & (gz + step < LINE)

    for c in range(CHUNKS):
        for k, step in enumerate(steps):
            pl.when(reaches(step))(
                lambda c=c, k=k, step=step: line_copy(c, gz, gz + step, z_send.at[c, k]).start()
            )

    for b in range(blocks):
        if b % 4:
            dequant(b)

    def vertical(c):
        src = kv[c].at[(1 - row) * (blocks - 1)]
        return copy(src, cbuf[c].at[2 * SLOTS], v_send.at[c], v_recv.at[c], other)

    for c in range(CHUNKS):
        vertical(c).start()

    def local(k):
        return pltpu.make_async_copy(heard.at[k], heard_s.at[k], req_local.at[k])

    def listen(k, device):
        ask(k, device).wait_recv()
        local(k).start()
        local(k).wait()

    listen(0, partner)
    pl.when(has_left)(lambda: listen(1, left))
    pl.when(has_right)(lambda: listen(2, right))

    def side_copy(c, side, device):
        base = SLOTS * (1 - side)
        return copy(
            csend[c].at[pl.ds(side * SLOTS, 2)], cbuf[c].at[pl.ds(base, 2)],
            c_send.at[c, side], c_recv.at[c, 1 - side], device,
        )

    def edge_copy(c, side, device):
        base = SLOTS * (1 - side)
        return copy(
            csend[c].at[side * SLOTS + 2], cbuf[c].at[base + 2],
            e_send.at[c, side], e_recv.at[c, 1 - side], device,
        )

    def send_sides(c):
        for side, exists, edge, device in (
            (0, has_left, col == 1, left), (1, has_right, col == cols - 2, right),
        ):
            @pl.when(exists)
            def _():
                at = 4 + (0 if side == 1 else SLOTS)
                k = 1 if side == 0 else 2
                for j in range(2):
                    csend[c][side * SLOTS + j] = kv[c][heard_s[k, 0, at + j]]
                side_copy(c, side, device).start()

            @pl.when(edge)
            def _():
                at = 4 + (0 if side == 1 else SLOTS)
                k = 1 if side == 0 else 2
                csend[c][side * SLOTS + 2] = kv[c][heard_s[k, 0, at + 2]]
                edge_copy(c, side, device).start()

    def forward(c):
        @pl.when(gz == 1)
        def _():
            line_copy(c, 3, 1, z_send.at[c, 0]).wait_recv()
            line_copy(c, 3, 0, f_send.at[c]).start()

        @pl.when(gz == 2)
        def _():
            line_copy(c, 0, 2, z_send.at[c, 0]).wait_recv()
            line_copy(c, 0, 3, f_send.at[c]).start()

    def partner_copy(c):
        return copy(psend[c], pbuf[c], p_send.at[c], p_recv.at[c], partner)

    def send_partner(c):
        for source in range(LINE):
            taken = ((gz == 1) & (source == 3)) | ((gz == 2) & (source == 0))
            pl.when((gz != source) & jnp.logical_not(taken))(
                lambda: line_copy(c, source, gz, z_send.at[c, 0]).wait_recv()
            )
        for i in range(4):
            psend[c][i] = zbuf[c][heard_s[0, 0, i]]
        partner_copy(c).start()

    def wait_inputs(c):
        partner_copy(c).wait_recv()
        vertical(c).wait_recv()
        pl.when(has_left)(lambda: side_copy(c, 1, left).wait_recv())
        pl.when(has_right)(lambda: side_copy(c, 0, right).wait_recv())
        pl.when(col == cols - 1)(lambda: edge_copy(c, 1, left).wait_recv())
        pl.when(col == 0)(lambda: edge_copy(c, 0, right).wait_recv())

    def attend(c):
        for i in range(4):
            kv[c][blocks + i] = cbuf[c][places[i]]
            kv[c][blocks + 4 + i] = jnp.where(
                places[8 + i] == 1, pbuf[c][i], zbuf[c][places[4 + i]]
            )
        factor = HEAD_DIM**-0.5 * math.log2(math.e)

        def tile(t, carry):
            rows = pl.ds(pl.multiple_of(t * QUERY_TILE, QUERY_TILE), QUERY_TILE)
            for h in range(width // HEAD_DIM):
                lanes = slice(h * HEAD_DIM, (h + 1) * HEAD_DIM)
                whole = slice(c * width + h * HEAD_DIM, c * width + (h + 1) * HEAD_DIM)
                keys = kv[c][:, 0, :, lanes].reshape(-1, HEAD_DIM)
                values = kv[c][:, 1, :, lanes].reshape(-1, HEAD_DIM)
                dots = lax.dot_general(
                    q_ref[rows, whole], keys, (((1,), (1,)), ((), ())),
                    preferred_element_type=jnp.float32,
                )
                top = jnp.max(dots, axis=-1, keepdims=True)
                weights = jnp.exp2((dots - top) * factor)
                total = jnp.sum(weights, axis=-1, keepdims=True)
                blended = jnp.dot(
                    weights.astype(jnp.bfloat16), values, preferred_element_type=jnp.float32
                )
                out_ref[rows, whole] = (blended / total).astype(jnp.bfloat16)
            return carry

        lax.fori_loop(0, q_ref.shape[0] // QUERY_TILE, tile, 0)

    for c in range(CHUNKS):
        send_sides(c)
    for c in range(CHUNKS):
        forward(c)
        send_partner(c)
        if c:
            wait_inputs(c - 1)
            attend(c - 1)
    wait_inputs(CHUNKS - 1)
    attend(CHUNKS - 1)

    ask(0, partner).wait_send()
    pl.when(has_left)(lambda: ask(2, left).wait_send())
    pl.when(has_right)(lambda: ask(1, right).wait_send())
    for c in range(CHUNKS):
        for k, step in enumerate(steps):
            pl.when(reaches(step))(
                lambda c=c, k=k, step=step: line_copy(c, gz, gz, z_send.at[c, k]).wait_send()
            )
        pl.when((gz == 1) | (gz == 2))(lambda: line_copy(c, 0, 0, f_send.at[c]).wait_send())
        partner_copy(c).wait_send()
        vertical(c).wait_send()
        pl.when(has_left)(lambda: side_copy(c, 0, left).wait_send())
        pl.when(has_right)(lambda: side_copy(c, 1, right).wait_send())
        pl.when(col == 1)(lambda: edge_copy(c, 0, left).wait_send())
        pl.when(col == cols - 2)(lambda: edge_copy(c, 1, right).wait_send())


def per_device(queries, key_mant, key_exp, value_mant, value_exp, cycle_list, dilated_list):
    blocks, _, block, features = queries.shape
    groups = key_exp.shape[2]
    cols = lax.axis_size("col")
    distant = blocks // 4
    width = features // CHUNKS
    member = lax.axis_index("col") // (cols // DILATION_TILES)
    asked, places = request_tables(cycle_list[0, 0], dilated_list[0, 0], blocks, member)
    vmem = pl.BlockSpec(memory_space=pltpu.VMEM)

    def buffers(slots):
        return [pltpu.VMEM((slots, 2, block, width), jnp.bfloat16)] * CHUNKS

    dma = pltpu.SemaphoreType.DMA
    tokens = blocks * block
    out = pl.pallas_call(
        functools.partial(kernel, cols, blocks),
        out_shape=jax.ShapeDtypeStruct((tokens, features), jnp.bfloat16),
        in_specs=[pl.BlockSpec(memory_space=pltpu.SMEM)] + [vmem] * 6,
        out_specs=vmem,
        scratch_shapes=[
            *buffers(blocks + 8), *buffers(LINE * distant), *buffers(4),
            *buffers(2 * SLOTS + 1), *buffers(4), *buffers(2 * SLOTS),
            pltpu.VMEM((3, 8, 128), jnp.int32), pltpu.SMEM((3, 8, 128), jnp.int32),
            dma((3,)), dma((3,)), dma((3,)),
            dma((CHUNKS, 4)), dma((CHUNKS, LINE)), dma((CHUNKS,)),
            dma((CHUNKS,)), dma((CHUNKS,)),
            dma((CHUNKS, 2)), dma((CHUNKS, 2)), dma((CHUNKS, 2)), dma((CHUNKS, 2)),
            dma((CHUNKS,)), dma((CHUNKS,)),
        ],
        compiler_params=pltpu.CompilerParams(
            collective_id=0, has_side_effects=True, vmem_limit_bytes=50 * 2**20
        ),
        cost_estimate=pl.CostEstimate(
            flops=8 * tokens * tokens * features, bytes_accessed=10 * tokens * features,
            transcendentals=2 * tokens * tokens * HEADS,
        ),
    )(
        places, queries.reshape(tokens, features),
        key_mant.reshape(blocks, block, features), key_exp.reshape(blocks, groups, features),
        value_mant.reshape(blocks, block, features), value_exp.reshape(blocks, groups, features),
        asked,
    )
    return out.reshape(queries.shape)


def solution(mesh):
    split = P(("groups", "row"), "col", None, None)
    lists = P(("groups", "row"), "col", None)
    return jax.shard_map(
        per_device, mesh=mesh, in_specs=(split,) * 5 + (lists,) * 2, out_specs=split,
        check_vma=False,
    )
```

```python
import functools
import math

import jax
import jax.numpy as jnp
from jax import lax
from jax.experimental import pallas as pl
from jax.experimental.pallas import tpu as pltpu
from jax.sharding import PartitionSpec as P

HEADS = 12
HEAD_DIM = 128
DILATION_TILES = 8
LINE = DILATION_TILES // 2
CHUNK_HEADS = (1, 2, 2, 2, 2, 2, 1)
CHUNKS = len(CHUNK_HEADS)
STARTS = tuple(sum(CHUNK_HEADS[:c]) * HEAD_DIM for c in range(CHUNKS))
WIDTHS = tuple(n * HEAD_DIM for n in CHUNK_HEADS)
AHEAD = 3
QUERY_TILE = 256
SLOTS = 3
MESH = pl.DeviceIdType.MESH


def side_entries(entries, low, high):
    found, rank = [], jnp.int32(0)
    for entry in entries:
        hit = (entry >= low) & (entry < high)
        found.append((hit, rank, entry - low))
        rank = rank + hit.astype(jnp.int32)
    return found


def slot_rows(found, slots):
    return [
        sum(jnp.where(hit & (rank == slot), place, 0) for hit, rank, place in found)
        for slot in range(slots)
    ]


def line_place(entry, member, distant):
    hop = lax.div(entry, distant) + 1
    source = lax.rem(member + hop, DILATION_TILES)
    place = lax.div(source, 2) * distant + lax.rem(entry, distant)
    return place, lax.rem(hop, 2) == 1


def kernel(cols, blocks, cycle, dilated, q_hbm, km_hbm, ke_hbm, vm_hbm, ve_hbm, out_ref, *scratch):
    kv = scratch[0:CHUNKS]
    zbuf = scratch[CHUNKS : 2 * CHUNKS]
    pbuf = scratch[2 * CHUNKS : 3 * CHUNKS]
    cbuf = scratch[3 * CHUNKS : 4 * CHUNKS]
    psend = scratch[4 * CHUNKS : 5 * CHUNKS]
    csend = scratch[5 * CHUNKS : 6 * CHUNKS]
    (q_ref, km_ref, ke_ref, vm_ref, ve_ref, in_sem, asked, heard, heard_s, req_send, req_recv, req_local, z_send, z_recv, f_send, p_send, p_recv,
     c_send, c_recv, e_send, e_recv, v_send, v_recv) = scratch[6 * CHUNKS :]
    block = kv[0].shape[-2]
    groups = ke_ref.shape[1]
    distant = blocks // 4
    spacing = cols // DILATION_TILES

    def fetch(src, dst, k):
        return pltpu.make_async_copy(src, dst, in_sem.at[k])

    pairs = ((km_hbm, km_ref), (vm_hbm, vm_ref))
    exponents = [fetch(ke_hbm, ke_ref, 0), fetch(ve_hbm, ve_ref, 1)]
    near = [
        fetch(src.at[4 * r], dst.at[4 * r], 2 + 2 * r + k)
        for r in range(distant) for k, (src, dst) in enumerate(pairs)
    ]
    far = [
        fetch(src.at[pl.ds(4 * r + 1, 3)], dst.at[pl.ds(4 * r + 1, 3)], 2 + 2 * (distant + r) + k)
        for r in range(distant) for k, (src, dst) in enumerate(pairs)
    ]
    queries = fetch(q_hbm, q_ref, 2 + 4 * distant)
    for part in (*exponents, *near, *far, queries):
        part.start()

    col = lax.axis_index("col")
    row = lax.axis_index("row")
    member, offset = col // spacing, lax.rem(col, spacing)
    gz, gy = member // 2, lax.rem(member, 2)

    def on_line(z):
        return {"col": (z * 2 + gy) * spacing + offset}

    partner = {"col": (gz * 2 + 1 - gy) * spacing + offset}
    left, right = {"col": col - 1}, {"col": col + 1}
    other = {"row": 1 - row}
    has_left, has_right = col > 0, col < cols - 1

    barrier = pltpu.get_barrier_semaphore()

    def greet(device):
        pl.semaphore_signal(barrier, inc=1, device_id=device, device_id_type=MESH)

    for z in range(LINE):
        pl.when(gz != z)(functools.partial(greet, on_line(z)))
    greet(partner)
    greet(other)
    pl.when(has_left)(functools.partial(greet, left))
    pl.when(has_right)(functools.partial(greet, right))

    def dequant(b):
        for which, (mant, expo) in enumerate(((km_ref, ke_ref), (vm_ref, ve_ref))):
            factor = lax.shift_left(jnp.int32(1), expo[b] + 8).astype(jnp.float32) * (2.0**-8)
            size = block // groups
            parts = [
                mant[b, g * size : (g + 1) * size, :].astype(jnp.float32) * factor[g : g + 1, :]
                for g in range(groups)
            ]
            full = jnp.concatenate(parts, axis=0).astype(jnp.bfloat16)
            for c in range(CHUNKS):
                kv[c][b, which] = full[:, STARTS[c] : STARTS[c] + WIDTHS[c]]

    lane = lax.broadcasted_iota(jnp.int32, asked.shape, 1)
    numbers = [cycle[i] for i in range(4)] + [dilated[i] for i in range(4)]
    asked[...] = sum(jnp.where(lane == i, number, 0) for i, number in enumerate(numbers))
    for part in (*exponents, *near):
        part.wait()
    for r in range(distant):
        dequant(4 * r)
        for c in range(CHUNKS):
            zbuf[c][gz * distant + r] = kv[c][4 * r]

    pl.semaphore_wait(barrier, LINE + 1 + has_left.astype(jnp.int32) + has_right.astype(jnp.int32))

    def copy(src, dst, send, recv, device):
        return pltpu.make_async_remote_copy(
            src_ref=src, dst_ref=dst, send_sem=send, recv_sem=recv,
            device_id=device, device_id_type=MESH,
        )

    def ask(k, device):
        return copy(asked, heard.at[k], req_send.at[k], req_recv.at[k], device)

    ask(0, partner).start()
    pl.when(has_left)(lambda: ask(2, left).start())
    pl.when(has_right)(lambda: ask(1, right).start())

    def line_copy(c, source, z, sem):
        part = zbuf[c].at[pl.ds(source * distant, distant)]
        return copy(part, part, sem, z_recv.at[c, source], on_line(z))

    steps = (1, -1, 2, -2)

    def reaches(step):
        return (gz + step >= 0) & (gz + step < LINE)

    def send_line(c):
        for k, step in enumerate(steps):
            pl.when(reaches(step))(
                lambda k=k, step=step: line_copy(c, gz, gz + step, z_send.at[c, k]).start()
            )

    for c in range(AHEAD):
        send_line(c)
    for part in far:
        part.wait()
    for b in range(blocks):
        if b % 4:
            dequant(b)

    def vertical(c):
        src = kv[c].at[(1 - row) * (blocks - 1)]
        return copy(src, cbuf[c].at[2 * SLOTS], v_send.at[c], v_recv.at[c], other)

    def local(k):
        return pltpu.make_async_copy(heard.at[k], heard_s.at[k], req_local.at[k])

    def listen(k, device):
        ask(k, device).wait_recv()
        local(k).start()
        local(k).wait()

    listen(0, partner)
    pl.when(has_left)(lambda: listen(1, left))
    pl.when(has_right)(lambda: listen(2, right))

    def side_copy(c, side, device):
        base = SLOTS * (1 - side)
        return copy(
            csend[c].at[pl.ds(side * SLOTS, 2)], cbuf[c].at[pl.ds(base, 2)],
            c_send.at[c, side], c_recv.at[c, 1 - side], device,
        )

    def edge_copy(c, side, device):
        base = SLOTS * (1 - side)
        return copy(
            csend[c].at[side * SLOTS + 2], cbuf[c].at[base + 2],
            e_send.at[c, side], e_recv.at[c, 1 - side], device,
        )

    sides = ((0, has_left, col == 1, left), (1, has_right, col == cols - 2, right))

    def send_sides(c):
        vertical(c).start()
        for side, exists, edge, device in sides:
            low = 2 + blocks * (1 - side)

            @pl.when(exists)
            def _():
                entries = [heard_s[1 + side, 0, i] for i in range(4)]
                rows = slot_rows(side_entries(entries, low, low + blocks), SLOTS)
                for j in range(2):
                    csend[c][side * SLOTS + j] = kv[c][rows[j]]
                side_copy(c, side, device).start()

                @pl.when(edge)
                def _():
                    csend[c][side * SLOTS + 2] = kv[c][rows[2]]
                    edge_copy(c, side, device).start()

    def forward(c):
        @pl.when(gz == 1)
        def _():
            line_copy(c, 3, 1, z_send.at[c, 0]).wait_recv()
            line_copy(c, 3, 0, f_send.at[c]).start()

        @pl.when(gz == 2)
        def _():
            line_copy(c, 0, 2, z_send.at[c, 0]).wait_recv()
            line_copy(c, 0, 3, f_send.at[c]).start()

    def partner_copy(c):
        return copy(psend[c], pbuf[c], p_send.at[c], p_recv.at[c], partner)

    def send_partner(c):
        for source in range(LINE):
            taken = ((gz == 1) & (source == 3)) | ((gz == 2) & (source == 0))
            pl.when((gz != source) & jnp.logical_not(taken))(
                lambda: line_copy(c, source, gz, z_send.at[c, 0]).wait_recv()
            )
        for i in range(4):
            place, _ = line_place(heard_s[0, 0, 4 + i], gz * 2 + 1 - gy, distant)
            psend[c][i] = zbuf[c][place]
        partner_copy(c).start()

    def wait_inputs(c):
        partner_copy(c).wait_recv()
        vertical(c).wait_recv()
        pl.when(has_left)(lambda: side_copy(c, 1, left).wait_recv())
        pl.when(has_right)(lambda: side_copy(c, 0, right).wait_recv())
        pl.when(col == cols - 1)(lambda: edge_copy(c, 1, left).wait_recv())
        pl.when(col == 0)(lambda: edge_copy(c, 0, right).wait_recv())

    entries = [cycle[i] for i in range(4)]
    lefts = side_entries(entries, 2, 2 + blocks)
    rights = side_entries(entries, 2 + blocks, 2 + 2 * blocks)
    cycle_places = [
        jnp.where(a[0], a[1], jnp.where(b[0], SLOTS + b[1], 2 * SLOTS))
        for a, b in zip(lefts, rights)
    ]

    def attend(c):
        for i in range(4):
            kv[c][blocks + i] = cbuf[c][cycle_places[i]]
            place, crossing = line_place(dilated[i], member, distant)
            kv[c][blocks + 4 + i] = jnp.where(crossing, pbuf[c][i], zbuf[c][place])
        factor = HEAD_DIM**-0.5 * math.log2(math.e)

        def tile(t, carry):
            rows = pl.ds(pl.multiple_of(t * QUERY_TILE, QUERY_TILE), QUERY_TILE)
            for h in range(CHUNK_HEADS[c]):
                lanes = slice(h * HEAD_DIM, (h + 1) * HEAD_DIM)
                whole = slice(STARTS[c] + h * HEAD_DIM, STARTS[c] + (h + 1) * HEAD_DIM)
                keys = kv[c][:, 0, :, lanes].reshape(-1, HEAD_DIM)
                values = kv[c][:, 1, :, lanes].reshape(-1, HEAD_DIM)
                dots = lax.dot_general(
                    q_ref[rows, whole], keys, (((1,), (1,)), ((), ())),
                    preferred_element_type=jnp.float32,
                )
                top = jnp.max(dots, axis=-1, keepdims=True)
                weights = jnp.exp2((dots - top) * factor)
                total = jnp.sum(weights, axis=-1, keepdims=True)
                blended = jnp.dot(
                    weights.astype(jnp.bfloat16), values, preferred_element_type=jnp.float32
                )
                out_ref[rows, whole] = (blended / total).astype(jnp.bfloat16)
            return carry

        lax.fori_loop(0, q_ref.shape[0] // QUERY_TILE, tile, 0)

    for c in range(AHEAD):
        send_sides(c)
    queries.wait()
    for c in range(CHUNKS):
        forward(c)
        send_partner(c)
        if c + AHEAD < CHUNKS:
            send_line(c + AHEAD)
            send_sides(c + AHEAD)
        if c:
            wait_inputs(c - 1)
            attend(c - 1)
    wait_inputs(CHUNKS - 1)
    attend(CHUNKS - 1)

    ask(0, partner).wait_send()
    pl.when(has_left)(lambda: ask(2, left).wait_send())
    pl.when(has_right)(lambda: ask(1, right).wait_send())
    for c in range(CHUNKS):
        for k, step in enumerate(steps):
            pl.when(reaches(step))(
                lambda c=c, k=k, step=step: line_copy(c, gz, gz, z_send.at[c, k]).wait_send()
            )
        pl.when((gz == 1) | (gz == 2))(lambda: line_copy(c, 0, 0, f_send.at[c]).wait_send())
        partner_copy(c).wait_send()
        vertical(c).wait_send()
        pl.when(has_left)(lambda: side_copy(c, 0, left).wait_send())
        pl.when(has_right)(lambda: side_copy(c, 1, right).wait_send())
        pl.when(col == 1)(lambda: edge_copy(c, 0, left).wait_send())
        pl.when(col == cols - 2)(lambda: edge_copy(c, 1, right).wait_send())


def per_device(queries, key_mant, key_exp, value_mant, value_exp, cycle_list, dilated_list):
    blocks, _, block, features = queries.shape
    groups = key_exp.shape[2]
    cols = lax.axis_size("col")
    distant = blocks // 4
    vmem = pltpu.VMEM
    smem = pl.BlockSpec(memory_space=pltpu.SMEM)
    anywhere = pl.BlockSpec(memory_space=pl.ANY)

    def buffers(slots):
        return [vmem((slots, 2, block, width), jnp.bfloat16) for width in WIDTHS]

    dma = pltpu.SemaphoreType.DMA
    tokens = blocks * block
    out = pl.pallas_call(
        functools.partial(kernel, cols, blocks),
        out_shape=jax.ShapeDtypeStruct((tokens, features), jnp.bfloat16),
        in_specs=[smem] * 2 + [anywhere] * 5,
        out_specs=pl.BlockSpec(memory_space=vmem),
        scratch_shapes=[
            *buffers(blocks + 8), *buffers(LINE * distant), *buffers(4),
            *buffers(2 * SLOTS + 1), *buffers(4), *buffers(2 * SLOTS),
            vmem((tokens, features), jnp.bfloat16),
            *[
                part
                for _ in range(2)
                for part in (
                    vmem((blocks, block, features), jnp.bfloat16),
                    vmem((blocks, groups, features), jnp.int32),
                )
            ],
            dma((3 + 4 * distant,)), vmem((8, 128), jnp.int32),
            pltpu.VMEM((3, 8, 128), jnp.int32), pltpu.SMEM((3, 8, 128), jnp.int32),
            dma((3,)), dma((3,)), dma((3,)),
            dma((CHUNKS, 4)), dma((CHUNKS, LINE)), dma((CHUNKS,)),
            dma((CHUNKS,)), dma((CHUNKS,)),
            dma((CHUNKS, 2)), dma((CHUNKS, 2)), dma((CHUNKS, 2)), dma((CHUNKS, 2)),
            dma((CHUNKS,)), dma((CHUNKS,)),
        ],
        compiler_params=pltpu.CompilerParams(
            collective_id=0, has_side_effects=True, vmem_limit_bytes=60 * 2**20
        ),
        cost_estimate=pl.CostEstimate(
            flops=8 * tokens * tokens * features, bytes_accessed=10 * tokens * features,
            transcendentals=2 * tokens * tokens * HEADS,
        ),
    )(
        cycle_list.reshape(-1), dilated_list.reshape(-1), queries.reshape(tokens, features),
        key_mant.reshape(blocks, block, features), key_exp.reshape(blocks, groups, features),
        value_mant.reshape(blocks, block, features), value_exp.reshape(blocks, groups, features),
    )
    return out.reshape(queries.shape)


def solution(mesh):
    split = P(("groups", "row"), "col", None, None)
    lists = P(("groups", "row"), "col", None)
    return jax.shard_map(
        per_device, mesh=mesh, in_specs=(split,) * 5 + (lists,) * 2, out_specs=split,
        check_vma=False,
    )
```

```python
import functools
import math

import jax
import jax.numpy as jnp
from jax import lax
from jax.experimental import pallas as pl
from jax.experimental.pallas import tpu as pltpu
from jax.sharding import PartitionSpec as P

HEADS = 12
HEAD_DIM = 128
DILATION_TILES = 8
LINE = DILATION_TILES // 2
CHUNK_HEADS = (1, 2, 2, 2, 2, 2, 1)
CHUNKS = len(CHUNK_HEADS)
STARTS = tuple(sum(CHUNK_HEADS[:c]) * HEAD_DIM for c in range(CHUNKS))
WIDTHS = tuple(n * HEAD_DIM for n in CHUNK_HEADS)
AHEAD = 3
DIRECT_CHUNKS = 2
QUERY_TILE = 256
SLOTS = 3
MESH = pl.DeviceIdType.MESH


def side_entries(entries, low, high):
    found, rank = [], jnp.int32(0)
    for entry in entries:
        hit = (entry >= low) & (entry < high)
        found.append((hit, rank, entry - low))
        rank = rank + hit.astype(jnp.int32)
    return found


def slot_rows(found, slots):
    return [
        sum(jnp.where(hit & (rank == slot), place, 0) for hit, rank, place in found)
        for slot in range(slots)
    ]


def line_place(entry, member, distant):
    hop = lax.div(entry, distant) + 1
    source = lax.rem(member + hop, DILATION_TILES)
    place = lax.div(source, 2) * distant + lax.rem(entry, distant)
    return place, lax.rem(hop, 2) == 1


def merges(cols, c):
    return cols == DILATION_TILES and c >= DIRECT_CHUNKS


def kernel(cols, blocks, cycle, dilated, q_hbm, km_hbm, ke_hbm, vm_hbm, ve_hbm, out_ref, *scratch):
    kv = scratch[0:CHUNKS]
    zbuf = scratch[CHUNKS : 2 * CHUNKS]
    pbuf = scratch[2 * CHUNKS : 3 * CHUNKS]
    cbuf = scratch[3 * CHUNKS : 4 * CHUNKS]
    psend = scratch[4 * CHUNKS : 5 * CHUNKS]
    csend = scratch[5 * CHUNKS : 6 * CHUNKS]
    dsend = scratch[6 * CHUNKS : 7 * CHUNKS]
    dbuf = scratch[7 * CHUNKS : 8 * CHUNKS]
    (q_ref, km_ref, ke_ref, vm_ref, ve_ref, in_sem, asked, heard, heard_s, req_send, req_recv, req_local, z_send, z_recv, f_send, p_send, p_recv,
     c_send, c_recv, e_send, e_recv, v_send, v_recv, d_send, d_recv) = scratch[8 * CHUNKS :]
    block = kv[0].shape[-2]
    groups = ke_ref.shape[1]
    distant = blocks // 4
    spacing = cols // DILATION_TILES

    merged = [merges(cols, c) for c in range(CHUNKS)]

    def fetch(src, dst, k):
        return pltpu.make_async_copy(src, dst, in_sem.at[k])

    pairs = ((km_hbm, km_ref), (vm_hbm, vm_ref))
    exponents = [fetch(ke_hbm, ke_ref, 0), fetch(ve_hbm, ve_ref, 1)]
    near = [
        fetch(src.at[4 * r], dst.at[4 * r], 2 + 2 * r + k)
        for r in range(distant) for k, (src, dst) in enumerate(pairs)
    ]
    far = [
        fetch(src.at[pl.ds(4 * r + 1, 3)], dst.at[pl.ds(4 * r + 1, 3)], 2 + 2 * (distant + r) + k)
        for r in range(distant) for k, (src, dst) in enumerate(pairs)
    ]
    queries = fetch(q_hbm, q_ref, 2 + 4 * distant)
    for part in (*exponents, *near, *far, queries):
        part.start()

    col = lax.axis_index("col")
    row = lax.axis_index("row")
    member, offset = col // spacing, lax.rem(col, spacing)
    gz, gy = member // 2, lax.rem(member, 2)

    def on_line(z):
        return {"col": (z * 2 + gy) * spacing + offset}

    partner = {"col": (gz * 2 + 1 - gy) * spacing + offset}
    left, right = {"col": col - 1}, {"col": col + 1}
    other = {"row": 1 - row}
    has_left, has_right = col > 0, col < cols - 1

    barrier = pltpu.get_barrier_semaphore()

    def greet(device):
        pl.semaphore_signal(barrier, inc=1, device_id=device, device_id_type=MESH)

    for z in range(LINE):
        pl.when(gz != z)(functools.partial(greet, on_line(z)))
    greet(partner)
    greet(other)
    pl.when(has_left)(functools.partial(greet, left))
    pl.when(has_right)(functools.partial(greet, right))

    def dequant(b):
        for which, (mant, expo) in enumerate(((km_ref, ke_ref), (vm_ref, ve_ref))):
            factor = lax.shift_left(jnp.int32(1), expo[b] + 8).astype(jnp.float32) * (2.0**-8)
            size = block // groups
            parts = [
                mant[b, g * size : (g + 1) * size, :].astype(jnp.float32) * factor[g : g + 1, :]
                for g in range(groups)
            ]
            full = jnp.concatenate(parts, axis=0).astype(jnp.bfloat16)
            for c in range(CHUNKS):
                kv[c][b, which] = full[:, STARTS[c] : STARTS[c] + WIDTHS[c]]

    lane = lax.broadcasted_iota(jnp.int32, asked.shape, 1)
    numbers = [cycle[i] for i in range(4)] + [dilated[i] for i in range(4)]
    asked[...] = sum(jnp.where(lane == i, number, 0) for i, number in enumerate(numbers))
    for part in (*exponents, *near):
        part.wait()
    for r in range(distant):
        dequant(4 * r)
        for c in range(CHUNKS):
            zbuf[c][gz * distant + r] = kv[c][4 * r]

    pl.semaphore_wait(barrier, LINE + 1 + has_left.astype(jnp.int32) + has_right.astype(jnp.int32))

    def copy(src, dst, send, recv, device):
        return pltpu.make_async_remote_copy(
            src_ref=src, dst_ref=dst, send_sem=send, recv_sem=recv,
            device_id=device, device_id_type=MESH,
        )

    def ask(k, device):
        return copy(asked, heard.at[k], req_send.at[k], req_recv.at[k], device)

    ask(0, partner).start()
    pl.when(has_left)(lambda: ask(2, left).start())
    pl.when(has_right)(lambda: ask(1, right).start())

    def line_copy(c, source, z, sem):
        part = zbuf[c].at[pl.ds(source * distant, distant)]
        return copy(part, part, sem, z_recv.at[c, source], on_line(z))

    steps = (1, -1, 2, -2)

    def reaches(step):
        return (gz + step >= 0) & (gz + step < LINE)

    def send_line(c):
        for k, step in enumerate(steps):
            pl.when(reaches(step))(
                lambda k=k, step=step: line_copy(c, gz, gz + step, z_send.at[c, k]).start()
            )

    for c in range(AHEAD):
        send_line(c)
    for part in far:
        part.wait()
    for b in range(blocks):
        if b % 4:
            dequant(b)

    def vertical(c):
        src = kv[c].at[(1 - row) * (blocks - 1)]
        return copy(src, cbuf[c].at[cbuf[c].shape[0] - 1], v_send.at[c], v_recv.at[c], other)

    def local(k):
        return pltpu.make_async_copy(heard.at[k], heard_s.at[k], req_local.at[k])

    def listen(k, device):
        ask(k, device).wait_recv()
        local(k).start()
        local(k).wait()

    listen(0, partner)
    pl.when(has_left)(lambda: listen(1, left))
    pl.when(has_right)(lambda: listen(2, right))

    def side_copy(c, side, device):
        base = SLOTS * (1 - side)
        return copy(
            csend[c].at[pl.ds(side * SLOTS, 2)], cbuf[c].at[pl.ds(base, 2)],
            c_send.at[c, side], c_recv.at[c, 1 - side], device,
        )

    def edge_copy(c, side, device):
        base = SLOTS * (1 - side)
        return copy(
            csend[c].at[side * SLOTS + 2], cbuf[c].at[base + 2],
            e_send.at[c, side], e_recv.at[c, 1 - side], device,
        )

    sides = ((0, has_left, col == 1, left), (1, has_right, col == cols - 2, right))

    diagonal_step = 2 * gy - 1
    gives = (gz + diagonal_step >= 0) & (gz + diagonal_step < LINE)
    takes = (gz - diagonal_step >= 0) & (gz - diagonal_step < LINE)

    def diagonal(c):
        return copy(dsend[c], dbuf[c], d_send.at[c], d_recv.at[c], on_line(gz + diagonal_step))

    def send_sides(c):
        vertical(c).start()
        if merged[c]:

            @pl.when(gives)
            def _():
                low = 2 + blocks * (1 - gy)
                entries = [
                    jnp.where(gy == 0, heard_s[1, 0, i], heard_s[2, 0, i]) for i in range(4)
                ]
                rows = slot_rows(side_entries(entries, low, low + blocks), 2)
                for j in range(2):
                    dsend[c][j] = kv[c][rows[j]]
                diagonal(c).start()

            return
        for side, exists, edge, device in sides:
            low = 2 + blocks * (1 - side)

            @pl.when(exists)
            def _():
                entries = [heard_s[1 + side, 0, i] for i in range(4)]
                rows = slot_rows(side_entries(entries, low, low + blocks), SLOTS)
                for j in range(2):
                    csend[c][side * SLOTS + j] = kv[c][rows[j]]
                side_copy(c, side, device).start()

                @pl.when(edge)
                def _():
                    csend[c][side * SLOTS + 2] = kv[c][rows[2]]
                    edge_copy(c, side, device).start()

    def forward(c):
        @pl.when(gz == 1)
        def _():
            line_copy(c, 3, 1, z_send.at[c, 0]).wait_recv()
            line_copy(c, 3, 0, f_send.at[c]).start()

        @pl.when(gz == 2)
        def _():
            line_copy(c, 0, 2, z_send.at[c, 0]).wait_recv()
            line_copy(c, 0, 3, f_send.at[c]).start()

    def partner_copy(c):
        return copy(psend[c], pbuf[c], p_send.at[c], p_recv.at[c], partner)

    def send_partner(c):
        for source in range(LINE):
            taken = ((gz == 1) & (source == 3)) | ((gz == 2) & (source == 0))
            pl.when((gz != source) & jnp.logical_not(taken))(
                lambda: line_copy(c, source, gz, z_send.at[c, 0]).wait_recv()
            )
        for i in range(4):
            place, _ = line_place(heard_s[0, 0, 4 + i], gz * 2 + 1 - gy, distant)
            psend[c][i] = zbuf[c][place]
        if merged[c]:
            pl.when(takes)(lambda: diagonal(c).wait_recv())
            entries = [heard_s[0, 0, i] for i in range(4)]
            own_low, far_low = 2 + blocks * gy, 2 + blocks * (1 - gy)
            own = side_entries(entries, own_low, own_low + blocks)
            far = side_entries(entries, far_low, far_low + blocks)
            across = side_entries(entries, 2, 2 + 2 * blocks)
            for j in range(SLOTS):
                here, row_at, far_at = jnp.bool_(False), jnp.int32(0), jnp.int32(0)
                for o, f, a in zip(own, far, across):
                    chosen = a[0] & (a[1] == j)
                    here = here | (chosen & o[0])
                    row_at = row_at + jnp.where(chosen & o[0], o[2], 0)
                    far_at = far_at + jnp.where(chosen & f[0], f[1], 0)
                psend[c][4 + j] = jnp.where(here, kv[c][row_at], dbuf[c][far_at])
        partner_copy(c).start()

    def wait_inputs(c):
        partner_copy(c).wait_recv()
        vertical(c).wait_recv()
        if merged[c]:
            return
        pl.when(has_left)(lambda: side_copy(c, 1, left).wait_recv())
        pl.when(has_right)(lambda: side_copy(c, 0, right).wait_recv())
        pl.when(col == cols - 1)(lambda: edge_copy(c, 1, left).wait_recv())
        pl.when(col == 0)(lambda: edge_copy(c, 0, right).wait_recv())

    entries = [cycle[i] for i in range(4)]
    lefts = side_entries(entries, 2, 2 + blocks)
    rights = side_entries(entries, 2 + blocks, 2 + 2 * blocks)
    cycle_places = [
        jnp.where(a[0], a[1], jnp.where(b[0], SLOTS + b[1], 2 * SLOTS))
        for a, b in zip(lefts, rights)
    ]
    acrosses = side_entries(entries, 2, 2 + 2 * blocks)

    def attend(c):
        for i in range(4):
            if merged[c]:
                across, rank, _ = acrosses[i]
                met = pbuf[c][4 + jnp.where(across, rank, 0)]
                kv[c][blocks + i] = jnp.where(across, met, cbuf[c][0])
            else:
                kv[c][blocks + i] = cbuf[c][cycle_places[i]]
            place, crossing = line_place(dilated[i], member, distant)
            kv[c][blocks + 4 + i] = jnp.where(crossing, pbuf[c][i], zbuf[c][place])
        factor = HEAD_DIM**-0.5 * math.log2(math.e)

        def tile(t, carry):
            rows = pl.ds(pl.multiple_of(t * QUERY_TILE, QUERY_TILE), QUERY_TILE)
            for h in range(CHUNK_HEADS[c]):
                lanes = slice(h * HEAD_DIM, (h + 1) * HEAD_DIM)
                whole = slice(STARTS[c] + h * HEAD_DIM, STARTS[c] + (h + 1) * HEAD_DIM)
                keys = kv[c][:, 0, :, lanes].reshape(-1, HEAD_DIM)
                values = kv[c][:, 1, :, lanes].reshape(-1, HEAD_DIM)
                dots = lax.dot_general(
                    q_ref[rows, whole], keys, (((1,), (1,)), ((), ())),
                    preferred_element_type=jnp.float32,
                )
                top = jnp.max(dots, axis=-1, keepdims=True)
                weights = jnp.exp2((dots - top) * factor)
                total = jnp.sum(weights, axis=-1, keepdims=True)
                blended = jnp.dot(
                    weights.astype(jnp.bfloat16), values, preferred_element_type=jnp.float32
                )
                out_ref[rows, whole] = (blended / total).astype(jnp.bfloat16)
            return carry

        lax.fori_loop(0, q_ref.shape[0] // QUERY_TILE, tile, 0)

    for c in range(AHEAD):
        send_sides(c)
    queries.wait()
    for c in range(CHUNKS):
        forward(c)
        send_partner(c)
        if c + AHEAD < CHUNKS:
            send_line(c + AHEAD)
            send_sides(c + AHEAD)
        if c:
            wait_inputs(c - 1)
            attend(c - 1)
    wait_inputs(CHUNKS - 1)
    attend(CHUNKS - 1)

    ask(0, partner).wait_send()
    pl.when(has_left)(lambda: ask(2, left).wait_send())
    pl.when(has_right)(lambda: ask(1, right).wait_send())
    for c in range(CHUNKS):
        for k, step in enumerate(steps):
            pl.when(reaches(step))(
                lambda c=c, k=k, step=step: line_copy(c, gz, gz, z_send.at[c, k]).wait_send()
            )
        pl.when((gz == 1) | (gz == 2))(lambda: line_copy(c, 0, 0, f_send.at[c]).wait_send())
        partner_copy(c).wait_send()
        vertical(c).wait_send()
        if merged[c]:
            pl.when(gives)(lambda: diagonal(c).wait_send())
            continue
        pl.when(has_left)(lambda: side_copy(c, 0, left).wait_send())
        pl.when(has_right)(lambda: side_copy(c, 1, right).wait_send())
        pl.when(col == 1)(lambda: edge_copy(c, 0, left).wait_send())
        pl.when(col == cols - 2)(lambda: edge_copy(c, 1, right).wait_send())


def per_device(queries, key_mant, key_exp, value_mant, value_exp, cycle_list, dilated_list):
    blocks, _, block, features = queries.shape
    groups = key_exp.shape[2]
    cols = lax.axis_size("col")
    distant = blocks // 4
    vmem = pltpu.VMEM
    smem = pl.BlockSpec(memory_space=pltpu.SMEM)
    anywhere = pl.BlockSpec(memory_space=pl.ANY)

    def buffers(slots, merged_slots=None):
        slots_of = [
            slots if merged_slots is None or not merges(cols, c) else merged_slots
            for c in range(CHUNKS)
        ]
        return [
            vmem((count, 2, block, width), jnp.bfloat16)
            for count, width in zip(slots_of, WIDTHS)
        ]

    dma = pltpu.SemaphoreType.DMA
    tokens = blocks * block
    out = pl.pallas_call(
        functools.partial(kernel, cols, blocks),
        out_shape=jax.ShapeDtypeStruct((tokens, features), jnp.bfloat16),
        in_specs=[smem] * 2 + [anywhere] * 5,
        out_specs=pl.BlockSpec(memory_space=vmem),
        scratch_shapes=[
            *buffers(blocks + 8), *buffers(LINE * distant), *buffers(4, 4 + SLOTS),
            *buffers(2 * SLOTS + 1, 1), *buffers(4, 4 + SLOTS), *buffers(2 * SLOTS, 1),
            *buffers(1, 2), *buffers(1, 2),
            vmem((tokens, features), jnp.bfloat16),
            *[
                part
                for _ in range(2)
                for part in (
                    vmem((blocks, block, features), jnp.bfloat16),
                    vmem((blocks, groups, features), jnp.int32),
                )
            ],
            dma((3 + 4 * distant,)), vmem((8, 128), jnp.int32),
            pltpu.VMEM((3, 8, 128), jnp.int32), pltpu.SMEM((3, 8, 128), jnp.int32),
            dma((3,)), dma((3,)), dma((3,)),
            dma((CHUNKS, 4)), dma((CHUNKS, LINE)), dma((CHUNKS,)),
            dma((CHUNKS,)), dma((CHUNKS,)),
            dma((CHUNKS, 2)), dma((CHUNKS, 2)), dma((CHUNKS, 2)), dma((CHUNKS, 2)),
            dma((CHUNKS,)), dma((CHUNKS,)), dma((CHUNKS,)), dma((CHUNKS,)),
        ],
        compiler_params=pltpu.CompilerParams(
            collective_id=0, has_side_effects=True, vmem_limit_bytes=57 * 2**20
        ),
        cost_estimate=pl.CostEstimate(
            flops=8 * tokens * tokens * features, bytes_accessed=10 * tokens * features,
            transcendentals=2 * tokens * tokens * HEADS,
        ),
    )(
        cycle_list.reshape(-1), dilated_list.reshape(-1), queries.reshape(tokens, features),
        key_mant.reshape(blocks, block, features), key_exp.reshape(blocks, groups, features),
        value_mant.reshape(blocks, block, features), value_exp.reshape(blocks, groups, features),
    )
    return out.reshape(queries.shape)


def solution(mesh):
    split = P(("groups", "row"), "col", None, None)
    lists = P(("groups", "row"), "col", None)
    return jax.shard_map(
        per_device, mesh=mesh, in_specs=(split,) * 5 + (lists,) * 2, out_specs=split,
        check_vma=False,
    )
```

```python
import functools
import math

import jax
import jax.numpy as jnp
from jax import lax
from jax.experimental import pallas as pl
from jax.experimental.pallas import tpu as pltpu
from jax.sharding import PartitionSpec as P

HEADS = 12
HEAD_DIM = 128
DILATION_TILES = 8
LINE = DILATION_TILES // 2
CHUNK_HEADS = (2, 2, 2, 2, 2, 1, 1)
CHUNKS = len(CHUNK_HEADS)
STARTS = tuple(sum(CHUNK_HEADS[:c]) * HEAD_DIM for c in range(CHUNKS))
WIDTHS = tuple(n * HEAD_DIM for n in CHUNK_HEADS)
AHEAD = 4
PARTNER_LAG = 1
ATTEND_LAG = 3
QUERY_TILE = 256
SLOTS = 3
MESH = pl.DeviceIdType.MESH


def side_entries(entries, low, high):
    found, rank = [], jnp.int32(0)
    for entry in entries:
        hit = (entry >= low) & (entry < high)
        found.append((hit, rank, entry - low))
        rank = rank + hit.astype(jnp.int32)
    return found


def slot_rows(found, slots):
    return [
        sum(jnp.where(hit & (rank == slot), place, 0) for hit, rank, place in found)
        for slot in range(slots)
    ]


def line_place(entry, member, distant):
    hop = lax.div(entry, distant) + 1
    source = lax.rem(member + hop, DILATION_TILES)
    place = lax.div(source, 2) * distant + lax.rem(entry, distant)
    return place, lax.rem(hop, 2) == 1


def kernel(cols, blocks, cycle, dilated, q_hbm, km_hbm, ke_hbm, vm_hbm, ve_hbm, out_ref, *scratch):
    kv = scratch[0:CHUNKS]
    zbuf = scratch[CHUNKS : 2 * CHUNKS]
    pbuf = scratch[2 * CHUNKS : 3 * CHUNKS]
    cbuf = scratch[3 * CHUNKS : 4 * CHUNKS]
    psend = scratch[4 * CHUNKS : 5 * CHUNKS]
    csend = scratch[5 * CHUNKS : 6 * CHUNKS]
    (q_ref, km_ref, ke_ref, vm_ref, ve_ref, in_sem, asked, heard, heard_s, req_send, req_recv, req_local, z_send, z_recv, f_send, p_send, p_recv,
     c_send, c_recv, e_send, e_recv, v_send, v_recv) = scratch[6 * CHUNKS :]
    block = kv[0].shape[-2]
    groups = ke_ref.shape[1]
    distant = blocks // 4
    spacing = cols // DILATION_TILES

    def fetch(src, dst, k):
        return pltpu.make_async_copy(src, dst, in_sem.at[k])

    pairs = ((km_hbm, km_ref), (vm_hbm, vm_ref))
    exponents = [fetch(ke_hbm, ke_ref, 0), fetch(ve_hbm, ve_ref, 1)]
    near = [
        fetch(src.at[4 * r], dst.at[4 * r], 2 + 2 * r + k)
        for r in range(distant) for k, (src, dst) in enumerate(pairs)
    ]
    far = [
        fetch(src.at[pl.ds(4 * r + 1, 3)], dst.at[pl.ds(4 * r + 1, 3)], 2 + 2 * (distant + r) + k)
        for r in range(distant) for k, (src, dst) in enumerate(pairs)
    ]
    queries = fetch(q_hbm, q_ref, 2 + 4 * distant)
    for part in (*exponents, *near, *far, queries):
        part.start()

    col = lax.axis_index("col")
    row = lax.axis_index("row")
    member, offset = col // spacing, lax.rem(col, spacing)
    gz, gy = member // 2, lax.rem(member, 2)

    def on_line(z):
        return {"col": (z * 2 + gy) * spacing + offset}

    partner = {"col": (gz * 2 + 1 - gy) * spacing + offset}
    left, right = {"col": col - 1}, {"col": col + 1}
    other = {"row": 1 - row}
    has_left, has_right = col > 0, col < cols - 1

    barrier = pltpu.get_barrier_semaphore()

    def greet(device):
        pl.semaphore_signal(barrier, inc=1, device_id=device, device_id_type=MESH)

    for z in range(LINE):
        pl.when(gz != z)(functools.partial(greet, on_line(z)))
    greet(partner)
    greet(other)
    pl.when(has_left)(functools.partial(greet, left))
    pl.when(has_right)(functools.partial(greet, right))

    def dequant(b):
        for which, (mant, expo) in enumerate(((km_ref, ke_ref), (vm_ref, ve_ref))):
            factor = lax.shift_left(jnp.int32(1), expo[b] + 8).astype(jnp.float32) * (2.0**-8)
            size = block // groups
            parts = [
                mant[b, g * size : (g + 1) * size, :].astype(jnp.float32) * factor[g : g + 1, :]
                for g in range(groups)
            ]
            full = jnp.concatenate(parts, axis=0).astype(jnp.bfloat16)
            for c in range(CHUNKS):
                kv[c][b, which] = full[:, STARTS[c] : STARTS[c] + WIDTHS[c]]

    lane = lax.broadcasted_iota(jnp.int32, asked.shape, 1)
    numbers = [cycle[i] for i in range(4)] + [dilated[i] for i in range(4)]
    asked[...] = sum(jnp.where(lane == i, number, 0) for i, number in enumerate(numbers))
    for part in (*exponents, *near):
        part.wait()
    for r in range(distant):
        dequant(4 * r)
        for c in range(CHUNKS):
            zbuf[c][gz * distant + r] = kv[c][4 * r]

    pl.semaphore_wait(barrier, LINE + 1 + has_left.astype(jnp.int32) + has_right.astype(jnp.int32))

    def copy(src, dst, send, recv, device):
        return pltpu.make_async_remote_copy(
            src_ref=src, dst_ref=dst, send_sem=send, recv_sem=recv,
            device_id=device, device_id_type=MESH,
        )

    def ask(k, device):
        return copy(asked, heard.at[k], req_send.at[k], req_recv.at[k], device)

    ask(0, partner).start()
    pl.when(has_left)(lambda: ask(2, left).start())
    pl.when(has_right)(lambda: ask(1, right).start())

    def line_copy(c, source, z, sem):
        part = zbuf[c].at[pl.ds(source * distant, distant)]
        return copy(part, part, sem, z_recv.at[c, source], on_line(z))

    steps = (1, -1, 2, -2)

    def reaches(step):
        return (gz + step >= 0) & (gz + step < LINE)

    def send_line(c):
        for k, step in enumerate(steps):
            pl.when(reaches(step))(
                lambda k=k, step=step: line_copy(c, gz, gz + step, z_send.at[c, k]).start()
            )

    for c in range(AHEAD):
        send_line(c)
    for part in far:
        part.wait()
    for b in range(blocks):
        if b % 4:
            dequant(b)

    def vertical(c):
        src = kv[c].at[(1 - row) * (blocks - 1)]
        return copy(src, cbuf[c].at[2 * SLOTS], v_send.at[c], v_recv.at[c], other)

    def local(k):
        return pltpu.make_async_copy(heard.at[k], heard_s.at[k], req_local.at[k])

    def listen(k, device):
        ask(k, device).wait_recv()
        local(k).start()
        local(k).wait()

    listen(0, partner)
    pl.when(has_left)(lambda: listen(1, left))
    pl.when(has_right)(lambda: listen(2, right))

    def side_copy(c, side, device):
        base = SLOTS * (1 - side)
        return copy(
            csend[c].at[pl.ds(side * SLOTS, 2)], cbuf[c].at[pl.ds(base, 2)],
            c_send.at[c, side], c_recv.at[c, 1 - side], device,
        )

    def edge_copy(c, side, device):
        base = SLOTS * (1 - side)
        return copy(
            csend[c].at[side * SLOTS + 2], cbuf[c].at[base + 2],
            e_send.at[c, side], e_recv.at[c, 1 - side], device,
        )

    sides = ((0, has_left, col == 1, left), (1, has_right, col == cols - 2, right))

    def send_sides(c):
        vertical(c).start()
        for side, exists, edge, device in sides:
            low = 2 + blocks * (1 - side)

            @pl.when(exists)
            def _():
                entries = [heard_s[1 + side, 0, i] for i in range(4)]
                rows = slot_rows(side_entries(entries, low, low + blocks), SLOTS)
                for j in range(2):
                    csend[c][side * SLOTS + j] = kv[c][rows[j]]
                side_copy(c, side, device).start()

                @pl.when(edge)
                def _():
                    csend[c][side * SLOTS + 2] = kv[c][rows[2]]
                    edge_copy(c, side, device).start()

    def forward(c):
        @pl.when(gz == 1)
        def _():
            line_copy(c, 3, 1, z_send.at[c, 0]).wait_recv()
            line_copy(c, 3, 0, f_send.at[c]).start()

        @pl.when(gz == 2)
        def _():
            line_copy(c, 0, 2, z_send.at[c, 0]).wait_recv()
            line_copy(c, 0, 3, f_send.at[c]).start()

    def partner_copy(c):
        return copy(psend[c], pbuf[c], p_send.at[c], p_recv.at[c], partner)

    def send_partner(c):
        for source in range(LINE):
            taken = ((gz == 1) & (source == 3)) | ((gz == 2) & (source == 0))
            pl.when((gz != source) & jnp.logical_not(taken))(
                lambda: line_copy(c, source, gz, z_send.at[c, 0]).wait_recv()
            )
        for i in range(4):
            place, _ = line_place(heard_s[0, 0, 4 + i], gz * 2 + 1 - gy, distant)
            psend[c][i] = zbuf[c][place]
        partner_copy(c).start()

    def wait_inputs(c):
        partner_copy(c).wait_recv()
        vertical(c).wait_recv()
        pl.when(has_left)(lambda: side_copy(c, 1, left).wait_recv())
        pl.when(has_right)(lambda: side_copy(c, 0, right).wait_recv())
        pl.when(col == cols - 1)(lambda: edge_copy(c, 1, left).wait_recv())
        pl.when(col == 0)(lambda: edge_copy(c, 0, right).wait_recv())

    entries = [cycle[i] for i in range(4)]
    lefts = side_entries(entries, 2, 2 + blocks)
    rights = side_entries(entries, 2 + blocks, 2 + 2 * blocks)
    cycle_places = [
        jnp.where(a[0], a[1], jnp.where(b[0], SLOTS + b[1], 2 * SLOTS))
        for a, b in zip(lefts, rights)
    ]

    def attend(c):
        for i in range(4):
            kv[c][blocks + i] = cbuf[c][cycle_places[i]]
            place, crossing = line_place(dilated[i], member, distant)
            kv[c][blocks + 4 + i] = jnp.where(crossing, pbuf[c][i], zbuf[c][place])
        factor = HEAD_DIM**-0.5 * math.log2(math.e)

        def tile(t, carry):
            rows = pl.ds(pl.multiple_of(t * QUERY_TILE, QUERY_TILE), QUERY_TILE)
            for h in range(CHUNK_HEADS[c]):
                lanes = slice(h * HEAD_DIM, (h + 1) * HEAD_DIM)
                whole = slice(STARTS[c] + h * HEAD_DIM, STARTS[c] + (h + 1) * HEAD_DIM)
                keys = kv[c][:, 0, :, lanes].reshape(-1, HEAD_DIM)
                values = kv[c][:, 1, :, lanes].reshape(-1, HEAD_DIM)
                dots = lax.dot_general(
                    q_ref[rows, whole], keys, (((1,), (1,)), ((), ())),
                    preferred_element_type=jnp.float32,
                )
                top = jnp.max(dots, axis=-1, keepdims=True)
                weights = jnp.exp2((dots - top) * factor)
                total = jnp.sum(weights, axis=-1, keepdims=True)
                blended = jnp.dot(
                    weights.astype(jnp.bfloat16), values, preferred_element_type=jnp.float32
                )
                out_ref[rows, whole] = (blended / total).astype(jnp.bfloat16)
            return carry

        lax.fori_loop(0, q_ref.shape[0] // QUERY_TILE, tile, 0)

    for c in range(AHEAD):
        send_sides(c)
    queries.wait()
    for t in range(CHUNKS + ATTEND_LAG):
        if t < CHUNKS:
            forward(t)
        if t + AHEAD < CHUNKS:
            send_line(t + AHEAD)
            send_sides(t + AHEAD)
        if 0 <= t - PARTNER_LAG < CHUNKS:
            send_partner(t - PARTNER_LAG)
        if t >= ATTEND_LAG:
            wait_inputs(t - ATTEND_LAG)
            attend(t - ATTEND_LAG)

    ask(0, partner).wait_send()
    pl.when(has_left)(lambda: ask(2, left).wait_send())
    pl.when(has_right)(lambda: ask(1, right).wait_send())
    for c in range(CHUNKS):
        for k, step in enumerate(steps):
            pl.when(reaches(step))(
                lambda c=c, k=k, step=step: line_copy(c, gz, gz, z_send.at[c, k]).wait_send()
            )
        pl.when((gz == 1) | (gz == 2))(lambda: line_copy(c, 0, 0, f_send.at[c]).wait_send())
        partner_copy(c).wait_send()
        vertical(c).wait_send()
        pl.when(has_left)(lambda: side_copy(c, 0, left).wait_send())
        pl.when(has_right)(lambda: side_copy(c, 1, right).wait_send())
        pl.when(col == 1)(lambda: edge_copy(c, 0, left).wait_send())
        pl.when(col == cols - 2)(lambda: edge_copy(c, 1, right).wait_send())


def per_device(queries, key_mant, key_exp, value_mant, value_exp, cycle_list, dilated_list):
    blocks, _, block, features = queries.shape
    groups = key_exp.shape[2]
    cols = lax.axis_size("col")
    distant = blocks // 4
    vmem = pltpu.VMEM
    smem = pl.BlockSpec(memory_space=pltpu.SMEM)
    anywhere = pl.BlockSpec(memory_space=pl.ANY)

    def buffers(slots):
        return [vmem((slots, 2, block, width), jnp.bfloat16) for width in WIDTHS]

    dma = pltpu.SemaphoreType.DMA
    tokens = blocks * block
    out = pl.pallas_call(
        functools.partial(kernel, cols, blocks),
        out_shape=jax.ShapeDtypeStruct((tokens, features), jnp.bfloat16),
        in_specs=[smem] * 2 + [anywhere] * 5,
        out_specs=pl.BlockSpec(memory_space=vmem),
        scratch_shapes=[
            *buffers(blocks + 8), *buffers(LINE * distant), *buffers(4),
            *buffers(2 * SLOTS + 1), *buffers(4), *buffers(2 * SLOTS),
            vmem((tokens, features), jnp.bfloat16),
            *[
                part
                for _ in range(2)
                for part in (
                    vmem((blocks, block, features), jnp.bfloat16),
                    vmem((blocks, groups, features), jnp.int32),
                )
            ],
            dma((3 + 4 * distant,)), vmem((8, 128), jnp.int32),
            pltpu.VMEM((3, 8, 128), jnp.int32), pltpu.SMEM((3, 8, 128), jnp.int32),
            dma((3,)), dma((3,)), dma((3,)),
            dma((CHUNKS, 4)), dma((CHUNKS, LINE)), dma((CHUNKS,)),
            dma((CHUNKS,)), dma((CHUNKS,)),
            dma((CHUNKS, 2)), dma((CHUNKS, 2)), dma((CHUNKS, 2)), dma((CHUNKS, 2)),
            dma((CHUNKS,)), dma((CHUNKS,)),
        ],
        compiler_params=pltpu.CompilerParams(
            collective_id=0, has_side_effects=True, vmem_limit_bytes=60 * 2**20
        ),
        cost_estimate=pl.CostEstimate(
            flops=8 * tokens * tokens * features, bytes_accessed=10 * tokens * features,
            transcendentals=2 * tokens * tokens * HEADS,
        ),
    )(
        cycle_list.reshape(-1), dilated_list.reshape(-1), queries.reshape(tokens, features),
        key_mant.reshape(blocks, block, features), key_exp.reshape(blocks, groups, features),
        value_mant.reshape(blocks, block, features), value_exp.reshape(blocks, groups, features),
    )
    return out.reshape(queries.shape)


def solution(mesh):
    split = P(("groups", "row"), "col", None, None)
    lists = P(("groups", "row"), "col", None)
    return jax.shard_map(
        per_device, mesh=mesh, in_specs=(split,) * 5 + (lists,) * 2, out_specs=split,
        check_vma=False,
    )
```

```python
import functools
import math

import jax
import jax.numpy as jnp
from jax import lax
from jax.experimental import pallas as pl
from jax.experimental.pallas import tpu as pltpu
from jax.sharding import PartitionSpec as P

HEADS = 12
HEAD_DIM = 128
DILATION_TILES = 8
LINE = DILATION_TILES // 2
CHUNK_HEADS = (2, 2, 2, 2, 2, 1, 1)
CHUNKS = len(CHUNK_HEADS)
STARTS = tuple(sum(CHUNK_HEADS[:c]) * HEAD_DIM for c in range(CHUNKS))
WIDTHS = tuple(n * HEAD_DIM for n in CHUNK_HEADS)
AHEAD = 4
DIRECT_CHUNKS = 2
PARTNER_LAG = 1
ATTEND_LAG = 3
QUERY_TILE = 256
SLOTS = 3
MESH = pl.DeviceIdType.MESH


def side_entries(entries, low, high):
    found, rank = [], jnp.int32(0)
    for entry in entries:
        hit = (entry >= low) & (entry < high)
        found.append((hit, rank, entry - low))
        rank = rank + hit.astype(jnp.int32)
    return found


def slot_rows(found, slots):
    return [
        sum(jnp.where(hit & (rank == slot), place, 0) for hit, rank, place in found)
        for slot in range(slots)
    ]


def line_place(entry, member, distant):
    hop = lax.div(entry, distant) + 1
    source = lax.rem(member + hop, DILATION_TILES)
    place = lax.div(source, 2) * distant + lax.rem(entry, distant)
    return place, lax.rem(hop, 2) == 1


def merges(cols, c):
    return cols == DILATION_TILES and c >= DIRECT_CHUNKS


def kernel(cols, blocks, cycle, dilated, q_hbm, km_hbm, ke_hbm, vm_hbm, ve_hbm, out_ref, *scratch):
    kv = scratch[0:CHUNKS]
    zbuf = scratch[CHUNKS : 2 * CHUNKS]
    pbuf = scratch[2 * CHUNKS : 3 * CHUNKS]
    cbuf = scratch[3 * CHUNKS : 4 * CHUNKS]
    psend = scratch[4 * CHUNKS : 5 * CHUNKS]
    csend = scratch[5 * CHUNKS : 6 * CHUNKS]
    dsend = scratch[6 * CHUNKS : 7 * CHUNKS]
    dbuf = scratch[7 * CHUNKS : 8 * CHUNKS]
    (q_ref, km_ref, ke_ref, vm_ref, ve_ref, in_sem, asked, heard, heard_s, req_send, req_recv, req_local, z_send, z_recv, f_send, p_send, p_recv,
     c_send, c_recv, e_send, e_recv, v_send, v_recv, d_send, d_recv) = scratch[8 * CHUNKS :]
    block = kv[0].shape[-2]
    groups = ke_ref.shape[1]
    distant = blocks // 4
    spacing = cols // DILATION_TILES

    merged = [merges(cols, c) for c in range(CHUNKS)]

    def fetch(src, dst, k):
        return pltpu.make_async_copy(src, dst, in_sem.at[k])

    pairs = ((km_hbm, km_ref), (vm_hbm, vm_ref))
    exponents = [fetch(ke_hbm, ke_ref, 0), fetch(ve_hbm, ve_ref, 1)]
    near = [
        fetch(src.at[4 * r], dst.at[4 * r], 2 + 2 * r + k)
        for r in range(distant) for k, (src, dst) in enumerate(pairs)
    ]
    far = [
        fetch(src.at[pl.ds(4 * r + 1, 3)], dst.at[pl.ds(4 * r + 1, 3)], 2 + 2 * (distant + r) + k)
        for r in range(distant) for k, (src, dst) in enumerate(pairs)
    ]
    queries = fetch(q_hbm, q_ref, 2 + 4 * distant)
    for part in (*exponents, *near, *far, queries):
        part.start()

    col = lax.axis_index("col")
    row = lax.axis_index("row")
    member, offset = col // spacing, lax.rem(col, spacing)
    gz, gy = member // 2, lax.rem(member, 2)

    def on_line(z):
        return {"col": (z * 2 + gy) * spacing + offset}

    partner = {"col": (gz * 2 + 1 - gy) * spacing + offset}
    left, right = {"col": col - 1}, {"col": col + 1}
    other = {"row": 1 - row}
    has_left, has_right = col > 0, col < cols - 1

    barrier = pltpu.get_barrier_semaphore()

    def greet(device):
        pl.semaphore_signal(barrier, inc=1, device_id=device, device_id_type=MESH)

    for z in range(LINE):
        pl.when(gz != z)(functools.partial(greet, on_line(z)))
    greet(partner)
    greet(other)
    pl.when(has_left)(functools.partial(greet, left))
    pl.when(has_right)(functools.partial(greet, right))

    def dequant(b):
        for which, (mant, expo) in enumerate(((km_ref, ke_ref), (vm_ref, ve_ref))):
            factor = lax.shift_left(jnp.int32(1), expo[b] + 8).astype(jnp.float32) * (2.0**-8)
            size = block // groups
            parts = [
                mant[b, g * size : (g + 1) * size, :].astype(jnp.float32) * factor[g : g + 1, :]
                for g in range(groups)
            ]
            full = jnp.concatenate(parts, axis=0).astype(jnp.bfloat16)
            for c in range(CHUNKS):
                kv[c][b, which] = full[:, STARTS[c] : STARTS[c] + WIDTHS[c]]

    lane = lax.broadcasted_iota(jnp.int32, asked.shape, 1)
    numbers = [cycle[i] for i in range(4)] + [dilated[i] for i in range(4)]
    asked[...] = sum(jnp.where(lane == i, number, 0) for i, number in enumerate(numbers))
    for part in (*exponents, *near):
        part.wait()
    for r in range(distant):
        dequant(4 * r)
        for c in range(CHUNKS):
            zbuf[c][gz * distant + r] = kv[c][4 * r]

    pl.semaphore_wait(barrier, LINE + 1 + has_left.astype(jnp.int32) + has_right.astype(jnp.int32))

    def copy(src, dst, send, recv, device):
        return pltpu.make_async_remote_copy(
            src_ref=src, dst_ref=dst, send_sem=send, recv_sem=recv,
            device_id=device, device_id_type=MESH,
        )

    def ask(k, device):
        return copy(asked, heard.at[k], req_send.at[k], req_recv.at[k], device)

    ask(0, partner).start()
    pl.when(has_left)(lambda: ask(2, left).start())
    pl.when(has_right)(lambda: ask(1, right).start())

    def line_copy(c, source, z, sem):
        part = zbuf[c].at[pl.ds(source * distant, distant)]
        return copy(part, part, sem, z_recv.at[c, source], on_line(z))

    steps = (1, -1, 2, -2)

    def reaches(step):
        return (gz + step >= 0) & (gz + step < LINE)

    def send_line(c):
        for k, step in enumerate(steps):
            pl.when(reaches(step))(
                lambda k=k, step=step: line_copy(c, gz, gz + step, z_send.at[c, k]).start()
            )

    for c in range(AHEAD):
        send_line(c)
    for part in far:
        part.wait()
    for b in range(blocks):
        if b % 4:
            dequant(b)

    def vertical(c):
        src = kv[c].at[(1 - row) * (blocks - 1)]
        return copy(src, cbuf[c].at[cbuf[c].shape[0] - 1], v_send.at[c], v_recv.at[c], other)

    def local(k):
        return pltpu.make_async_copy(heard.at[k], heard_s.at[k], req_local.at[k])

    def listen(k, device):
        ask(k, device).wait_recv()
        local(k).start()
        local(k).wait()

    listen(0, partner)
    pl.when(has_left)(lambda: listen(1, left))
    pl.when(has_right)(lambda: listen(2, right))

    def side_copy(c, side, device):
        base = SLOTS * (1 - side)
        return copy(
            csend[c].at[pl.ds(side * SLOTS, 2)], cbuf[c].at[pl.ds(base, 2)],
            c_send.at[c, side], c_recv.at[c, 1 - side], device,
        )

    def edge_copy(c, side, device):
        base = SLOTS * (1 - side)
        return copy(
            csend[c].at[side * SLOTS + 2], cbuf[c].at[base + 2],
            e_send.at[c, side], e_recv.at[c, 1 - side], device,
        )

    sides = ((0, has_left, col == 1, left), (1, has_right, col == cols - 2, right))

    diagonal_step = 2 * gy - 1
    gives = (gz + diagonal_step >= 0) & (gz + diagonal_step < LINE)
    takes = (gz - diagonal_step >= 0) & (gz - diagonal_step < LINE)

    def diagonal(c):
        return copy(dsend[c], dbuf[c], d_send.at[c], d_recv.at[c], on_line(gz + diagonal_step))

    def send_sides(c):
        vertical(c).start()
        if merged[c]:

            @pl.when(gives)
            def _():
                low = 2 + blocks * (1 - gy)
                entries = [
                    jnp.where(gy == 0, heard_s[1, 0, i], heard_s[2, 0, i]) for i in range(4)
                ]
                rows = slot_rows(side_entries(entries, low, low + blocks), 2)
                for j in range(2):
                    dsend[c][j] = kv[c][rows[j]]
                diagonal(c).start()

            return
        for side, exists, edge, device in sides:
            low = 2 + blocks * (1 - side)

            @pl.when(exists)
            def _():
                entries = [heard_s[1 + side, 0, i] for i in range(4)]
                rows = slot_rows(side_entries(entries, low, low + blocks), SLOTS)
                for j in range(2):
                    csend[c][side * SLOTS + j] = kv[c][rows[j]]
                side_copy(c, side, device).start()

                @pl.when(edge)
                def _():
                    csend[c][side * SLOTS + 2] = kv[c][rows[2]]
                    edge_copy(c, side, device).start()

    def forward(c):
        @pl.when(gz == 1)
        def _():
            line_copy(c, 3, 1, z_send.at[c, 0]).wait_recv()
            line_copy(c, 3, 0, f_send.at[c]).start()

        @pl.when(gz == 2)
        def _():
            line_copy(c, 0, 2, z_send.at[c, 0]).wait_recv()
            line_copy(c, 0, 3, f_send.at[c]).start()

    def merged_copy(c):
        return copy(
            csend[c], cbuf[c].at[pl.ds(0, SLOTS)], c_send.at[c, 0], c_recv.at[c, 0], partner
        )

    def send_merged(c):
        pl.when(takes)(lambda: diagonal(c).wait_recv())
        entries = [heard_s[0, 0, i] for i in range(4)]
        own_low, far_low = 2 + blocks * gy, 2 + blocks * (1 - gy)
        own = side_entries(entries, own_low, own_low + blocks)
        far = side_entries(entries, far_low, far_low + blocks)
        across = side_entries(entries, 2, 2 + 2 * blocks)
        for j in range(SLOTS):
            here, row_at, far_at = jnp.bool_(False), jnp.int32(0), jnp.int32(0)
            for o, f, a in zip(own, far, across):
                chosen = a[0] & (a[1] == j)
                here = here | (chosen & o[0])
                row_at = row_at + jnp.where(chosen & o[0], o[2], 0)
                far_at = far_at + jnp.where(chosen & f[0], f[1], 0)
            csend[c][j] = jnp.where(here, kv[c][row_at], dbuf[c][far_at])
        merged_copy(c).start()

    def partner_copy(c):
        return copy(psend[c], pbuf[c], p_send.at[c], p_recv.at[c], partner)

    def send_partner(c):
        for source in range(LINE):
            taken = ((gz == 1) & (source == 3)) | ((gz == 2) & (source == 0))
            pl.when((gz != source) & jnp.logical_not(taken))(
                lambda: line_copy(c, source, gz, z_send.at[c, 0]).wait_recv()
            )
        for i in range(4):
            place, _ = line_place(heard_s[0, 0, 4 + i], gz * 2 + 1 - gy, distant)
            psend[c][i] = zbuf[c][place]
        partner_copy(c).start()

    def wait_inputs(c):
        partner_copy(c).wait_recv()
        vertical(c).wait_recv()
        if merged[c]:
            merged_copy(c).wait_recv()
            return
        pl.when(has_left)(lambda: side_copy(c, 1, left).wait_recv())
        pl.when(has_right)(lambda: side_copy(c, 0, right).wait_recv())
        pl.when(col == cols - 1)(lambda: edge_copy(c, 1, left).wait_recv())
        pl.when(col == 0)(lambda: edge_copy(c, 0, right).wait_recv())

    entries = [cycle[i] for i in range(4)]
    lefts = side_entries(entries, 2, 2 + blocks)
    rights = side_entries(entries, 2 + blocks, 2 + 2 * blocks)
    cycle_places = [
        jnp.where(a[0], a[1], jnp.where(b[0], SLOTS + b[1], 2 * SLOTS))
        for a, b in zip(lefts, rights)
    ]
    merged_places = [
        jnp.where(hit, rank, SLOTS) for hit, rank, _ in side_entries(entries, 2, 2 + 2 * blocks)
    ]

    def attend(c):
        for i in range(4):
            kv[c][blocks + i] = cbuf[c][(merged_places if merged[c] else cycle_places)[i]]
            place, crossing = line_place(dilated[i], member, distant)
            kv[c][blocks + 4 + i] = jnp.where(crossing, pbuf[c][i], zbuf[c][place])
        factor = HEAD_DIM**-0.5 * math.log2(math.e)

        def tile(t, carry):
            rows = pl.ds(pl.multiple_of(t * QUERY_TILE, QUERY_TILE), QUERY_TILE)
            for h in range(CHUNK_HEADS[c]):
                lanes = slice(h * HEAD_DIM, (h + 1) * HEAD_DIM)
                whole = slice(STARTS[c] + h * HEAD_DIM, STARTS[c] + (h + 1) * HEAD_DIM)
                keys = kv[c][:, 0, :, lanes].reshape(-1, HEAD_DIM)
                values = kv[c][:, 1, :, lanes].reshape(-1, HEAD_DIM)
                dots = lax.dot_general(
                    q_ref[rows, whole], keys, (((1,), (1,)), ((), ())),
                    preferred_element_type=jnp.float32,
                )
                top = jnp.max(dots, axis=-1, keepdims=True)
                weights = jnp.exp2((dots - top) * factor)
                total = jnp.sum(weights, axis=-1, keepdims=True)
                blended = jnp.dot(
                    weights.astype(jnp.bfloat16), values, preferred_element_type=jnp.float32
                )
                out_ref[rows, whole] = (blended / total).astype(jnp.bfloat16)
            return carry

        lax.fori_loop(0, q_ref.shape[0] // QUERY_TILE, tile, 0)

    for c in range(AHEAD):
        send_sides(c)
    queries.wait()
    for t in range(CHUNKS + ATTEND_LAG):
        if t < CHUNKS:
            forward(t)
            if merged[t]:
                send_merged(t)
        if t + AHEAD < CHUNKS:
            send_line(t + AHEAD)
            send_sides(t + AHEAD)
        if 0 <= t - PARTNER_LAG < CHUNKS:
            send_partner(t - PARTNER_LAG)
        if t >= ATTEND_LAG:
            wait_inputs(t - ATTEND_LAG)
            attend(t - ATTEND_LAG)

    ask(0, partner).wait_send()
    pl.when(has_left)(lambda: ask(2, left).wait_send())
    pl.when(has_right)(lambda: ask(1, right).wait_send())
    for c in range(CHUNKS):
        for k, step in enumerate(steps):
            pl.when(reaches(step))(
                lambda c=c, k=k, step=step: line_copy(c, gz, gz, z_send.at[c, k]).wait_send()
            )
        pl.when((gz == 1) | (gz == 2))(lambda: line_copy(c, 0, 0, f_send.at[c]).wait_send())
        partner_copy(c).wait_send()
        vertical(c).wait_send()
        if merged[c]:
            pl.when(gives)(lambda: diagonal(c).wait_send())
            merged_copy(c).wait_send()
            continue
        pl.when(has_left)(lambda: side_copy(c, 0, left).wait_send())
        pl.when(has_right)(lambda: side_copy(c, 1, right).wait_send())
        pl.when(col == 1)(lambda: edge_copy(c, 0, left).wait_send())
        pl.when(col == cols - 2)(lambda: edge_copy(c, 1, right).wait_send())


def per_device(queries, key_mant, key_exp, value_mant, value_exp, cycle_list, dilated_list):
    blocks, _, block, features = queries.shape
    groups = key_exp.shape[2]
    cols = lax.axis_size("col")
    distant = blocks // 4
    vmem = pltpu.VMEM
    smem = pl.BlockSpec(memory_space=pltpu.SMEM)
    anywhere = pl.BlockSpec(memory_space=pl.ANY)

    def buffers(slots, merged_slots=None):
        slots_of = [
            slots if merged_slots is None or not merges(cols, c) else merged_slots
            for c in range(CHUNKS)
        ]
        return [
            vmem((count, 2, block, width), jnp.bfloat16)
            for count, width in zip(slots_of, WIDTHS)
        ]

    dma = pltpu.SemaphoreType.DMA
    tokens = blocks * block
    out = pl.pallas_call(
        functools.partial(kernel, cols, blocks),
        out_shape=jax.ShapeDtypeStruct((tokens, features), jnp.bfloat16),
        in_specs=[smem] * 2 + [anywhere] * 5,
        out_specs=pl.BlockSpec(memory_space=vmem),
        scratch_shapes=[
            *buffers(blocks + 8), *buffers(LINE * distant), *buffers(4),
            *buffers(2 * SLOTS + 1, SLOTS + 1), *buffers(4), *buffers(2 * SLOTS, SLOTS),
            *buffers(1, 2), *buffers(1, 2),
            vmem((tokens, features), jnp.bfloat16),
            *[
                part
                for _ in range(2)
                for part in (
                    vmem((blocks, block, features), jnp.bfloat16),
                    vmem((blocks, groups, features), jnp.int32),
                )
            ],
            dma((3 + 4 * distant,)), vmem((8, 128), jnp.int32),
            pltpu.VMEM((3, 8, 128), jnp.int32), pltpu.SMEM((3, 8, 128), jnp.int32),
            dma((3,)), dma((3,)), dma((3,)),
            dma((CHUNKS, 4)), dma((CHUNKS, LINE)), dma((CHUNKS,)),
            dma((CHUNKS,)), dma((CHUNKS,)),
            dma((CHUNKS, 2)), dma((CHUNKS, 2)), dma((CHUNKS, 2)), dma((CHUNKS, 2)),
            dma((CHUNKS,)), dma((CHUNKS,)), dma((CHUNKS,)), dma((CHUNKS,)),
        ],
        compiler_params=pltpu.CompilerParams(
            collective_id=0, has_side_effects=True, vmem_limit_bytes=60 * 2**20
        ),
        cost_estimate=pl.CostEstimate(
            flops=8 * tokens * tokens * features, bytes_accessed=10 * tokens * features,
            transcendentals=2 * tokens * tokens * HEADS,
        ),
    )(
        cycle_list.reshape(-1), dilated_list.reshape(-1), queries.reshape(tokens, features),
        key_mant.reshape(blocks, block, features), key_exp.reshape(blocks, groups, features),
        value_mant.reshape(blocks, block, features), value_exp.reshape(blocks, groups, features),
    )
    return out.reshape(queries.shape)


def solution(mesh):
    split = P(("groups", "row"), "col", None, None)
    lists = P(("groups", "row"), "col", None)
    return jax.shard_map(
        per_device, mesh=mesh, in_specs=(split,) * 5 + (lists,) * 2, out_specs=split,
        check_vma=False,
    )
```

```python
import functools
import math

import jax
import jax.numpy as jnp
from jax import lax
from jax.experimental import pallas as pl
from jax.experimental.pallas import tpu as pltpu
from jax.sharding import PartitionSpec as P

HEADS = 12
HEAD_DIM = 128
DILATION_TILES = 8
LINE = DILATION_TILES // 2
CHUNK_HEADS = (1,) * HEADS
CHUNKS = len(CHUNK_HEADS)
STARTS = tuple(sum(CHUNK_HEADS[:c]) * HEAD_DIM for c in range(CHUNKS))
WIDTHS = tuple(n * HEAD_DIM for n in CHUNK_HEADS)
AHEAD = 3
PARTNER_LAG = 1
ATTEND_LAG = 3
QUERY_TILE = 256
SLOTS = 3
MESH = pl.DeviceIdType.MESH


def side_entries(entries, low, high):
    found, rank = [], jnp.int32(0)
    for entry in entries:
        hit = (entry >= low) & (entry < high)
        found.append((hit, rank, entry - low))
        rank = rank + hit.astype(jnp.int32)
    return found


def slot_rows(found, slots):
    return [
        sum(jnp.where(hit & (rank == slot), place, 0) for hit, rank, place in found)
        for slot in range(slots)
    ]


def line_place(entry, member, distant):
    hop = lax.div(entry, distant) + 1
    source = lax.rem(member + hop, DILATION_TILES)
    place = lax.div(source, 2) * distant + lax.rem(entry, distant)
    return place, lax.rem(hop, 2) == 1


def kernel(cols, blocks, cycle, dilated, q_hbm, km_hbm, ke_hbm, vm_hbm, ve_hbm, out_ref, *scratch):
    kv = scratch[0:CHUNKS]
    zbuf = scratch[CHUNKS : 2 * CHUNKS]
    pbuf = scratch[2 * CHUNKS : 3 * CHUNKS]
    cbuf = scratch[3 * CHUNKS : 4 * CHUNKS]
    psend = scratch[4 * CHUNKS : 5 * CHUNKS]
    csend = scratch[5 * CHUNKS : 6 * CHUNKS]
    (q_ref, km_ref, ke_ref, vm_ref, ve_ref, in_sem, asked, heard, heard_s, req_send, req_recv, req_local, z_send, z_recv, f_send, p_send, p_recv,
     c_send, c_recv, e_send, e_recv, v_send, v_recv) = scratch[6 * CHUNKS :]
    block = kv[0].shape[-2]
    groups = ke_ref.shape[1]
    distant = blocks // 4
    spacing = cols // DILATION_TILES

    def fetch(src, dst, k):
        return pltpu.make_async_copy(src, dst, in_sem.at[k])

    pairs = ((km_hbm, km_ref), (vm_hbm, vm_ref))
    exponents = [fetch(ke_hbm, ke_ref, 0), fetch(ve_hbm, ve_ref, 1)]
    near = [
        fetch(src.at[4 * r], dst.at[4 * r], 2 + 2 * r + k)
        for r in range(distant) for k, (src, dst) in enumerate(pairs)
    ]
    far = [
        fetch(src.at[pl.ds(4 * r + 1, 3)], dst.at[pl.ds(4 * r + 1, 3)], 2 + 2 * (distant + r) + k)
        for r in range(distant) for k, (src, dst) in enumerate(pairs)
    ]
    queries = fetch(q_hbm, q_ref, 2 + 4 * distant)
    for part in (*exponents, *near, *far, queries):
        part.start()

    col = lax.axis_index("col")
    row = lax.axis_index("row")
    member, offset = col // spacing, lax.rem(col, spacing)
    gz, gy = member // 2, lax.rem(member, 2)

    def on_line(z):
        return {"col": (z * 2 + gy) * spacing + offset}

    partner = {"col": (gz * 2 + 1 - gy) * spacing + offset}
    left, right = {"col": col - 1}, {"col": col + 1}
    other = {"row": 1 - row}
    has_left, has_right = col > 0, col < cols - 1

    barrier = pltpu.get_barrier_semaphore()

    def greet(device):
        pl.semaphore_signal(barrier, inc=1, device_id=device, device_id_type=MESH)

    for z in range(LINE):
        pl.when(gz != z)(functools.partial(greet, on_line(z)))
    greet(partner)
    greet(other)
    pl.when(has_left)(functools.partial(greet, left))
    pl.when(has_right)(functools.partial(greet, right))

    def dequant(b):
        for which, (mant, expo) in enumerate(((km_ref, ke_ref), (vm_ref, ve_ref))):
            factor = lax.shift_left(jnp.int32(1), expo[b] + 8).astype(jnp.float32) * (2.0**-8)
            size = block // groups
            parts = [
                mant[b, g * size : (g + 1) * size, :].astype(jnp.float32) * factor[g : g + 1, :]
                for g in range(groups)
            ]
            full = jnp.concatenate(parts, axis=0).astype(jnp.bfloat16)
            for c in range(CHUNKS):
                kv[c][b, which] = full[:, STARTS[c] : STARTS[c] + WIDTHS[c]]

    lane = lax.broadcasted_iota(jnp.int32, asked.shape, 1)
    numbers = [cycle[i] for i in range(4)] + [dilated[i] for i in range(4)]
    asked[...] = sum(jnp.where(lane == i, number, 0) for i, number in enumerate(numbers))
    for part in (*exponents, *near):
        part.wait()
    for r in range(distant):
        dequant(4 * r)
        for c in range(CHUNKS):
            zbuf[c][gz * distant + r] = kv[c][4 * r]

    pl.semaphore_wait(barrier, LINE + 1 + has_left.astype(jnp.int32) + has_right.astype(jnp.int32))

    def copy(src, dst, send, recv, device):
        return pltpu.make_async_remote_copy(
            src_ref=src, dst_ref=dst, send_sem=send, recv_sem=recv,
            device_id=device, device_id_type=MESH,
        )

    def ask(k, device):
        return copy(asked, heard.at[k], req_send.at[k], req_recv.at[k], device)

    ask(0, partner).start()
    pl.when(has_left)(lambda: ask(2, left).start())
    pl.when(has_right)(lambda: ask(1, right).start())

    def line_copy(c, source, z, sem):
        part = zbuf[c].at[pl.ds(source * distant, distant)]
        return copy(part, part, sem, z_recv.at[c, source], on_line(z))

    steps = (2, -2, 1, -1)

    def reaches(step):
        return (gz + step >= 0) & (gz + step < LINE)

    def send_line(c):
        for k, step in enumerate(steps):
            pl.when(reaches(step))(
                lambda k=k, step=step: line_copy(c, gz, gz + step, z_send.at[c, k]).start()
            )

    for c in range(AHEAD):
        send_line(c)
    for part in far:
        part.wait()
    for b in range(blocks):
        if b % 4:
            dequant(b)

    def vertical(c):
        src = kv[c].at[(1 - row) * (blocks - 1)]
        return copy(src, cbuf[c].at[2 * SLOTS], v_send.at[c], v_recv.at[c], other)

    def local(k):
        return pltpu.make_async_copy(heard.at[k], heard_s.at[k], req_local.at[k])

    def listen(k, device):
        ask(k, device).wait_recv()
        local(k).start()
        local(k).wait()

    listen(0, partner)
    pl.when(has_left)(lambda: listen(1, left))
    pl.when(has_right)(lambda: listen(2, right))

    def side_copy(c, side, device):
        base = SLOTS * (1 - side)
        return copy(
            csend[c].at[pl.ds(side * SLOTS, 2)], cbuf[c].at[pl.ds(base, 2)],
            c_send.at[c, side], c_recv.at[c, 1 - side], device,
        )

    def edge_copy(c, side, device):
        base = SLOTS * (1 - side)
        return copy(
            csend[c].at[side * SLOTS + 2], cbuf[c].at[base + 2],
            e_send.at[c, side], e_recv.at[c, 1 - side], device,
        )

    sides = ((0, has_left, col == 1, left), (1, has_right, col == cols - 2, right))

    def send_sides(c):
        vertical(c).start()
        for side, exists, edge, device in sides:
            low = 2 + blocks * (1 - side)

            @pl.when(exists)
            def _():
                entries = [heard_s[1 + side, 0, i] for i in range(4)]
                rows = slot_rows(side_entries(entries, low, low + blocks), SLOTS)
                for j in range(2):
                    csend[c][side * SLOTS + j] = kv[c][rows[j]]
                side_copy(c, side, device).start()

                @pl.when(edge)
                def _():
                    csend[c][side * SLOTS + 2] = kv[c][rows[2]]
                    edge_copy(c, side, device).start()

    def forward(c):
        @pl.when(gz == 1)
        def _():
            line_copy(c, 3, 1, z_send.at[c, 0]).wait_recv()
            line_copy(c, 3, 0, f_send.at[c]).start()

        @pl.when(gz == 2)
        def _():
            line_copy(c, 0, 2, z_send.at[c, 0]).wait_recv()
            line_copy(c, 0, 3, f_send.at[c]).start()

    def partner_copy(c):
        return copy(psend[c], pbuf[c], p_send.at[c], p_recv.at[c], partner)

    def send_partner(c):
        for source in range(LINE):
            taken = ((gz == 1) & (source == 3)) | ((gz == 2) & (source == 0))
            pl.when((gz != source) & jnp.logical_not(taken))(
                lambda: line_copy(c, source, gz, z_send.at[c, 0]).wait_recv()
            )
        for i in range(4):
            place, _ = line_place(heard_s[0, 0, 4 + i], gz * 2 + 1 - gy, distant)
            psend[c][i] = zbuf[c][place]
        partner_copy(c).start()

    def wait_inputs(c):
        partner_copy(c).wait_recv()
        vertical(c).wait_recv()
        pl.when(has_left)(lambda: side_copy(c, 1, left).wait_recv())
        pl.when(has_right)(lambda: side_copy(c, 0, right).wait_recv())
        pl.when(col == cols - 1)(lambda: edge_copy(c, 1, left).wait_recv())
        pl.when(col == 0)(lambda: edge_copy(c, 0, right).wait_recv())

    entries = [cycle[i] for i in range(4)]
    lefts = side_entries(entries, 2, 2 + blocks)
    rights = side_entries(entries, 2 + blocks, 2 + 2 * blocks)
    cycle_places = [
        jnp.where(a[0], a[1], jnp.where(b[0], SLOTS + b[1], 2 * SLOTS))
        for a, b in zip(lefts, rights)
    ]

    def attend(c):
        for i in range(4):
            kv[c][blocks + i] = cbuf[c][cycle_places[i]]
            place, crossing = line_place(dilated[i], member, distant)
            kv[c][blocks + 4 + i] = jnp.where(crossing, pbuf[c][i], zbuf[c][place])
        factor = HEAD_DIM**-0.5 * math.log2(math.e)

        def tile(t, carry):
            rows = pl.ds(pl.multiple_of(t * QUERY_TILE, QUERY_TILE), QUERY_TILE)
            for h in range(CHUNK_HEADS[c]):
                lanes = slice(h * HEAD_DIM, (h + 1) * HEAD_DIM)
                whole = slice(STARTS[c] + h * HEAD_DIM, STARTS[c] + (h + 1) * HEAD_DIM)
                keys = kv[c][:, 0, :, lanes].reshape(-1, HEAD_DIM)
                values = kv[c][:, 1, :, lanes].reshape(-1, HEAD_DIM)
                dots = lax.dot_general(
                    q_ref[rows, whole], keys, (((1,), (1,)), ((), ())),
                    preferred_element_type=jnp.float32,
                )
                top = jnp.max(dots, axis=-1, keepdims=True)
                weights = jnp.exp2((dots - top) * factor)
                total = jnp.sum(weights, axis=-1, keepdims=True)
                blended = jnp.dot(
                    weights.astype(jnp.bfloat16), values, preferred_element_type=jnp.float32
                )
                out_ref[rows, whole] = (blended / total).astype(jnp.bfloat16)
            return carry

        lax.fori_loop(0, q_ref.shape[0] // QUERY_TILE, tile, 0)

    for c in range(AHEAD):
        send_sides(c)
    queries.wait()
    for t in range(CHUNKS + ATTEND_LAG):
        if t < CHUNKS:
            forward(t)
        if t + AHEAD < CHUNKS:
            send_line(t + AHEAD)
            send_sides(t + AHEAD)
        if 0 <= t - PARTNER_LAG < CHUNKS:
            send_partner(t - PARTNER_LAG)
        if t >= ATTEND_LAG:
            wait_inputs(t - ATTEND_LAG)
            attend(t - ATTEND_LAG)

    ask(0, partner).wait_send()
    pl.when(has_left)(lambda: ask(2, left).wait_send())
    pl.when(has_right)(lambda: ask(1, right).wait_send())
    for c in range(CHUNKS):
        for k, step in enumerate(steps):
            pl.when(reaches(step))(
                lambda c=c, k=k, step=step: line_copy(c, gz, gz, z_send.at[c, k]).wait_send()
            )
        pl.when((gz == 1) | (gz == 2))(lambda: line_copy(c, 0, 0, f_send.at[c]).wait_send())
        partner_copy(c).wait_send()
        vertical(c).wait_send()
        pl.when(has_left)(lambda: side_copy(c, 0, left).wait_send())
        pl.when(has_right)(lambda: side_copy(c, 1, right).wait_send())
        pl.when(col == 1)(lambda: edge_copy(c, 0, left).wait_send())
        pl.when(col == cols - 2)(lambda: edge_copy(c, 1, right).wait_send())


def per_device(queries, key_mant, key_exp, value_mant, value_exp, cycle_list, dilated_list):
    blocks, _, block, features = queries.shape
    groups = key_exp.shape[2]
    cols = lax.axis_size("col")
    distant = blocks // 4
    vmem = pltpu.VMEM
    smem = pl.BlockSpec(memory_space=pltpu.SMEM)
    anywhere = pl.BlockSpec(memory_space=pl.ANY)

    def buffers(slots):
        return [vmem((slots, 2, block, width), jnp.bfloat16) for width in WIDTHS]

    dma = pltpu.SemaphoreType.DMA
    tokens = blocks * block
    out = pl.pallas_call(
        functools.partial(kernel, cols, blocks),
        out_shape=jax.ShapeDtypeStruct((tokens, features), jnp.bfloat16),
        in_specs=[smem] * 2 + [anywhere] * 5,
        out_specs=pl.BlockSpec(memory_space=vmem),
        scratch_shapes=[
            *buffers(blocks + 8), *buffers(LINE * distant), *buffers(4),
            *buffers(2 * SLOTS + 1), *buffers(4), *buffers(2 * SLOTS),
            vmem((tokens, features), jnp.bfloat16),
            *[
                part
                for _ in range(2)
                for part in (
                    vmem((blocks, block, features), jnp.bfloat16),
                    vmem((blocks, groups, features), jnp.int32),
                )
            ],
            dma((3 + 4 * distant,)), vmem((8, 128), jnp.int32),
            pltpu.VMEM((3, 8, 128), jnp.int32), pltpu.SMEM((3, 8, 128), jnp.int32),
            dma((3,)), dma((3,)), dma((3,)),
            dma((CHUNKS, 4)), dma((CHUNKS, LINE)), dma((CHUNKS,)),
            dma((CHUNKS,)), dma((CHUNKS,)),
            dma((CHUNKS, 2)), dma((CHUNKS, 2)), dma((CHUNKS, 2)), dma((CHUNKS, 2)),
            dma((CHUNKS,)), dma((CHUNKS,)),
        ],
        compiler_params=pltpu.CompilerParams(
            collective_id=0, has_side_effects=True, vmem_limit_bytes=60 * 2**20
        ),
        cost_estimate=pl.CostEstimate(
            flops=8 * tokens * tokens * features, bytes_accessed=10 * tokens * features,
            transcendentals=2 * tokens * tokens * HEADS,
        ),
    )(
        cycle_list.reshape(-1), dilated_list.reshape(-1), queries.reshape(tokens, features),
        key_mant.reshape(blocks, block, features), key_exp.reshape(blocks, groups, features),
        value_mant.reshape(blocks, block, features), value_exp.reshape(blocks, groups, features),
    )
    return out.reshape(queries.shape)


def solution(mesh):
    split = P(("groups", "row"), "col", None, None)
    lists = P(("groups", "row"), "col", None)
    return jax.shard_map(
        per_device, mesh=mesh, in_specs=(split,) * 5 + (lists,) * 2, out_specs=split,
        check_vma=False,
    )
```

```python
import functools
import math

import jax
import jax.numpy as jnp
from jax import lax
from jax.experimental import pallas as pl
from jax.experimental.pallas import tpu as pltpu
from jax.sharding import PartitionSpec as P

HEADS = 12
HEAD_DIM = 128
DILATION_TILES = 8
LINE = DILATION_TILES // 2
CHUNK_HEADS = (1,) * HEADS
CHUNKS = len(CHUNK_HEADS)
STARTS = tuple(sum(CHUNK_HEADS[:c]) * HEAD_DIM for c in range(CHUNKS))
WIDTHS = tuple(n * HEAD_DIM for n in CHUNK_HEADS)
AHEAD = 3
SIDES_AHEAD = 6
PARTNER_LAG = 1
ATTEND_LAG = 3
QUERY_TILE = 256
SLOTS = 3
MESH = pl.DeviceIdType.MESH


def side_entries(entries, low, high):
    found, rank = [], jnp.int32(0)
    for entry in entries:
        hit = (entry >= low) & (entry < high)
        found.append((hit, rank, entry - low))
        rank = rank + hit.astype(jnp.int32)
    return found


def slot_rows(found, slots):
    return [
        sum(jnp.where(hit & (rank == slot), place, 0) for hit, rank, place in found)
        for slot in range(slots)
    ]


def line_place(entry, member, distant):
    hop = lax.div(entry, distant) + 1
    source = lax.rem(member + hop, DILATION_TILES)
    place = lax.div(source, 2) * distant + lax.rem(entry, distant)
    return place, lax.rem(hop, 2) == 1


def kernel(cols, blocks, cycle, dilated, q_hbm, km_hbm, ke_hbm, vm_hbm, ve_hbm, out_hbm, *scratch):
    kv = scratch[0:CHUNKS]
    zbuf = scratch[CHUNKS : 2 * CHUNKS]
    pbuf = scratch[2 * CHUNKS : 3 * CHUNKS]
    cbuf = scratch[3 * CHUNKS : 4 * CHUNKS]
    psend = scratch[4 * CHUNKS : 5 * CHUNKS]
    csend = scratch[5 * CHUNKS : 6 * CHUNKS]
    (out_ref, out_sem, q_ref, km_ref, ke_ref, vm_ref, ve_ref, in_sem, asked, heard, heard_s, req_send, req_recv, req_local, z_send, z_recv, f_send, p_send, p_recv,
     c_send, c_recv, e_send, e_recv, v_send, v_recv) = scratch[6 * CHUNKS :]
    block = kv[0].shape[-2]
    groups = ke_ref.shape[1]
    distant = blocks // 4
    spacing = cols // DILATION_TILES

    def fetch(src, dst, k):
        return pltpu.make_async_copy(src, dst, in_sem.at[k])

    pairs = ((km_hbm, km_ref), (vm_hbm, vm_ref))
    exponents = [fetch(ke_hbm, ke_ref, 0), fetch(ve_hbm, ve_ref, 1)]
    near = [
        fetch(src.at[4 * r], dst.at[4 * r], 2 + 2 * r + k)
        for r in range(distant) for k, (src, dst) in enumerate(pairs)
    ]
    far = [
        fetch(src.at[pl.ds(4 * r + 1, 3)], dst.at[pl.ds(4 * r + 1, 3)], 2 + 2 * (distant + r) + k)
        for r in range(distant) for k, (src, dst) in enumerate(pairs)
    ]
    queries = fetch(q_hbm, q_ref, 2 + 4 * distant)
    for part in (*exponents, *near, *far, queries):
        part.start()

    col = lax.axis_index("col")
    row = lax.axis_index("row")
    member, offset = col // spacing, lax.rem(col, spacing)
    gz, gy = member // 2, lax.rem(member, 2)

    def on_line(z):
        return {"col": (z * 2 + gy) * spacing + offset}

    partner = {"col": (gz * 2 + 1 - gy) * spacing + offset}
    left, right = {"col": col - 1}, {"col": col + 1}
    other = {"row": 1 - row}
    has_left, has_right = col > 0, col < cols - 1

    barrier = pltpu.get_barrier_semaphore()

    def greet(device):
        pl.semaphore_signal(barrier, inc=1, device_id=device, device_id_type=MESH)

    for z in range(LINE):
        pl.when(gz != z)(functools.partial(greet, on_line(z)))
    greet(partner)
    greet(other)
    pl.when(has_left)(functools.partial(greet, left))
    pl.when(has_right)(functools.partial(greet, right))

    def dequant(b):
        for which, (mant, expo) in enumerate(((km_ref, ke_ref), (vm_ref, ve_ref))):
            factor = lax.shift_left(jnp.int32(1), expo[b] + 8).astype(jnp.float32) * (2.0**-8)
            size = block // groups
            parts = [
                mant[b, g * size : (g + 1) * size, :].astype(jnp.float32) * factor[g : g + 1, :]
                for g in range(groups)
            ]
            full = jnp.concatenate(parts, axis=0).astype(jnp.bfloat16)
            for c in range(CHUNKS):
                kv[c][b, which] = full[:, STARTS[c] : STARTS[c] + WIDTHS[c]]

    lane = lax.broadcasted_iota(jnp.int32, asked.shape, 1)
    numbers = [cycle[i] for i in range(4)] + [dilated[i] for i in range(4)]
    asked[...] = sum(jnp.where(lane == i, number, 0) for i, number in enumerate(numbers))
    for part in (*exponents, *near):
        part.wait()
    for r in range(distant):
        dequant(4 * r)
        for c in range(CHUNKS):
            zbuf[c][gz * distant + r] = kv[c][4 * r]

    pl.semaphore_wait(barrier, LINE + 1 + has_left.astype(jnp.int32) + has_right.astype(jnp.int32))

    def copy(src, dst, send, recv, device):
        return pltpu.make_async_remote_copy(
            src_ref=src, dst_ref=dst, send_sem=send, recv_sem=recv,
            device_id=device, device_id_type=MESH,
        )

    def ask(k, device):
        return copy(asked, heard.at[k], req_send.at[k], req_recv.at[k], device)

    ask(0, partner).start()
    pl.when(has_left)(lambda: ask(2, left).start())
    pl.when(has_right)(lambda: ask(1, right).start())

    def line_copy(c, source, z, sem):
        part = zbuf[c].at[pl.ds(source * distant, distant)]
        return copy(part, part, sem, z_recv.at[c, source], on_line(z))

    steps = (2, -2, 1, -1)

    def reaches(step):
        return (gz + step >= 0) & (gz + step < LINE)

    def send_line(c):
        for k, step in enumerate(steps):
            pl.when(reaches(step))(
                lambda k=k, step=step: line_copy(c, gz, gz + step, z_send.at[c, k]).start()
            )

    for c in range(AHEAD):
        send_line(c)
    for part in far:
        part.wait()
    for b in range(blocks):
        if b % 4:
            dequant(b)

    def vertical(c):
        src = kv[c].at[(1 - row) * (blocks - 1)]
        return copy(src, cbuf[c].at[2 * SLOTS], v_send.at[c], v_recv.at[c], other)

    def local(k):
        return pltpu.make_async_copy(heard.at[k], heard_s.at[k], req_local.at[k])

    def listen(k, device):
        ask(k, device).wait_recv()
        local(k).start()
        local(k).wait()

    listen(0, partner)
    pl.when(has_left)(lambda: listen(1, left))
    pl.when(has_right)(lambda: listen(2, right))

    def side_copy(c, side, device):
        base = SLOTS * (1 - side)
        return copy(
            csend[c].at[pl.ds(side * SLOTS, 2)], cbuf[c].at[pl.ds(base, 2)],
            c_send.at[c, side], c_recv.at[c, 1 - side], device,
        )

    def edge_copy(c, side, device):
        base = SLOTS * (1 - side)
        return copy(
            csend[c].at[side * SLOTS + 2], cbuf[c].at[base + 2],
            e_send.at[c, side], e_recv.at[c, 1 - side], device,
        )

    sides = ((0, has_left, col == 1, left), (1, has_right, col == cols - 2, right))

    def send_sides(c):
        vertical(c).start()
        for side, exists, edge, device in sides:
            low = 2 + blocks * (1 - side)

            @pl.when(exists)
            def _():
                entries = [heard_s[1 + side, 0, i] for i in range(4)]
                rows = slot_rows(side_entries(entries, low, low + blocks), SLOTS)
                for j in range(2):
                    csend[c][side * SLOTS + j] = kv[c][rows[j]]
                side_copy(c, side, device).start()

                @pl.when(edge)
                def _():
                    csend[c][side * SLOTS + 2] = kv[c][rows[2]]
                    edge_copy(c, side, device).start()

    def forward(c):
        @pl.when(gz == 1)
        def _():
            line_copy(c, 3, 1, z_send.at[c, 0]).wait_recv()
            line_copy(c, 3, 0, f_send.at[c]).start()

        @pl.when(gz == 2)
        def _():
            line_copy(c, 0, 2, z_send.at[c, 0]).wait_recv()
            line_copy(c, 0, 3, f_send.at[c]).start()

    def partner_copy(c):
        return copy(psend[c], pbuf[c], p_send.at[c], p_recv.at[c], partner)

    def send_partner(c):
        for source in range(LINE):
            taken = ((gz == 1) & (source == 3)) | ((gz == 2) & (source == 0))
            pl.when((gz != source) & jnp.logical_not(taken))(
                lambda: line_copy(c, source, gz, z_send.at[c, 0]).wait_recv()
            )
        for i in range(4):
            place, _ = line_place(heard_s[0, 0, 4 + i], gz * 2 + 1 - gy, distant)
            psend[c][i] = zbuf[c][place]
        partner_copy(c).start()

    def wait_inputs(c):
        partner_copy(c).wait_recv()
        vertical(c).wait_recv()
        pl.when(has_left)(lambda: side_copy(c, 1, left).wait_recv())
        pl.when(has_right)(lambda: side_copy(c, 0, right).wait_recv())
        pl.when(col == cols - 1)(lambda: edge_copy(c, 1, left).wait_recv())
        pl.when(col == 0)(lambda: edge_copy(c, 0, right).wait_recv())

    entries = [cycle[i] for i in range(4)]
    lefts = side_entries(entries, 2, 2 + blocks)
    rights = side_entries(entries, 2 + blocks, 2 + 2 * blocks)
    cycle_places = [
        jnp.where(a[0], a[1], jnp.where(b[0], SLOTS + b[1], 2 * SLOTS))
        for a, b in zip(lefts, rights)
    ]

    def deliver(c):
        lanes = pl.ds(STARTS[c], WIDTHS[c])
        return pltpu.make_async_copy(out_ref.at[:, lanes], out_hbm.at[:, lanes], out_sem.at[c])

    def attend(c):
        for i in range(4):
            kv[c][blocks + i] = cbuf[c][cycle_places[i]]
            place, crossing = line_place(dilated[i], member, distant)
            kv[c][blocks + 4 + i] = jnp.where(crossing, pbuf[c][i], zbuf[c][place])
        factor = HEAD_DIM**-0.5 * math.log2(math.e)

        def tile(t, carry):
            rows = pl.ds(pl.multiple_of(t * QUERY_TILE, QUERY_TILE), QUERY_TILE)
            for h in range(CHUNK_HEADS[c]):
                lanes = slice(h * HEAD_DIM, (h + 1) * HEAD_DIM)
                whole = slice(STARTS[c] + h * HEAD_DIM, STARTS[c] + (h + 1) * HEAD_DIM)
                keys = kv[c][:, 0, :, lanes].reshape(-1, HEAD_DIM)
                values = kv[c][:, 1, :, lanes].reshape(-1, HEAD_DIM)
                dots = lax.dot_general(
                    q_ref[rows, whole], keys, (((1,), (1,)), ((), ())),
                    preferred_element_type=jnp.float32,
                )
                top = jnp.max(dots, axis=-1, keepdims=True)
                weights = jnp.exp2((dots - top) * factor)
                total = jnp.sum(weights, axis=-1, keepdims=True)
                blended = jnp.dot(
                    weights.astype(jnp.bfloat16), values, preferred_element_type=jnp.float32
                )
                out_ref[rows, whole] = (blended / total).astype(jnp.bfloat16)
            return carry

        lax.fori_loop(0, q_ref.shape[0] // QUERY_TILE, tile, 0)
        deliver(c).start()

    for c in range(SIDES_AHEAD):
        send_sides(c)
    queries.wait()
    for t in range(CHUNKS + ATTEND_LAG):
        if t < CHUNKS:
            forward(t)
        if t + AHEAD < CHUNKS:
            send_line(t + AHEAD)
        if t + SIDES_AHEAD < CHUNKS:
            send_sides(t + SIDES_AHEAD)
        if 0 <= t - PARTNER_LAG < CHUNKS:
            send_partner(t - PARTNER_LAG)
        if t >= ATTEND_LAG:
            wait_inputs(t - ATTEND_LAG)
            attend(t - ATTEND_LAG)

    ask(0, partner).wait_send()
    pl.when(has_left)(lambda: ask(2, left).wait_send())
    pl.when(has_right)(lambda: ask(1, right).wait_send())
    for c in range(CHUNKS):
        for k, step in enumerate(steps):
            pl.when(reaches(step))(
                lambda c=c, k=k, step=step: line_copy(c, gz, gz, z_send.at[c, k]).wait_send()
            )
        pl.when((gz == 1) | (gz == 2))(lambda: line_copy(c, 0, 0, f_send.at[c]).wait_send())
        deliver(c).wait()
        partner_copy(c).wait_send()
        vertical(c).wait_send()
        pl.when(has_left)(lambda: side_copy(c, 0, left).wait_send())
        pl.when(has_right)(lambda: side_copy(c, 1, right).wait_send())
        pl.when(col == 1)(lambda: edge_copy(c, 0, left).wait_send())
        pl.when(col == cols - 2)(lambda: edge_copy(c, 1, right).wait_send())


def per_device(queries, key_mant, key_exp, value_mant, value_exp, cycle_list, dilated_list):
    blocks, _, block, features = queries.shape
    groups = key_exp.shape[2]
    cols = lax.axis_size("col")
    distant = blocks // 4
    vmem = pltpu.VMEM
    smem = pl.BlockSpec(memory_space=pltpu.SMEM)
    anywhere = pl.BlockSpec(memory_space=pl.ANY)

    def buffers(slots):
        return [vmem((slots, 2, block, width), jnp.bfloat16) for width in WIDTHS]

    dma = pltpu.SemaphoreType.DMA
    tokens = blocks * block
    out = pl.pallas_call(
        functools.partial(kernel, cols, blocks),
        out_shape=jax.ShapeDtypeStruct((tokens, features), jnp.bfloat16),
        in_specs=[smem] * 2 + [anywhere] * 5,
        out_specs=anywhere,
        scratch_shapes=[
            *buffers(blocks + 8), *buffers(LINE * distant), *buffers(4),
            *buffers(2 * SLOTS + 1), *buffers(4), *buffers(2 * SLOTS),
            vmem((tokens, features), jnp.bfloat16), dma((CHUNKS,)),
            vmem((tokens, features), jnp.bfloat16),
            *[
                part
                for _ in range(2)
                for part in (
                    vmem((blocks, block, features), jnp.bfloat16),
                    vmem((blocks, groups, features), jnp.int32),
                )
            ],
            dma((3 + 4 * distant,)), vmem((8, 128), jnp.int32),
            pltpu.VMEM((3, 8, 128), jnp.int32), pltpu.SMEM((3, 8, 128), jnp.int32),
            dma((3,)), dma((3,)), dma((3,)),
            dma((CHUNKS, 4)), dma((CHUNKS, LINE)), dma((CHUNKS,)),
            dma((CHUNKS,)), dma((CHUNKS,)),
            dma((CHUNKS, 2)), dma((CHUNKS, 2)), dma((CHUNKS, 2)), dma((CHUNKS, 2)),
            dma((CHUNKS,)), dma((CHUNKS,)),
        ],
        compiler_params=pltpu.CompilerParams(
            collective_id=0, has_side_effects=True, vmem_limit_bytes=60 * 2**20
        ),
        cost_estimate=pl.CostEstimate(
            flops=8 * tokens * tokens * features, bytes_accessed=10 * tokens * features,
            transcendentals=2 * tokens * tokens * HEADS,
        ),
    )(
        cycle_list.reshape(-1), dilated_list.reshape(-1), queries.reshape(tokens, features),
        key_mant.reshape(blocks, block, features), key_exp.reshape(blocks, groups, features),
        value_mant.reshape(blocks, block, features), value_exp.reshape(blocks, groups, features),
    )
    return out.reshape(queries.shape)


def solution(mesh):
    split = P(("groups", "row"), "col", None, None)
    lists = P(("groups", "row"), "col", None)
    return jax.shard_map(
        per_device, mesh=mesh, in_specs=(split,) * 5 + (lists,) * 2, out_specs=split,
        check_vma=False,
    )
```

```python
import functools
import math

import jax
import jax.numpy as jnp
from jax import lax
from jax.experimental import pallas as pl
from jax.experimental.pallas import tpu as pltpu
from jax.sharding import PartitionSpec as P

HEADS = 12
HEAD_DIM = 128
DILATION_TILES = 8
LINE = DILATION_TILES // 2
CHUNK_HEADS = (1,) * HEADS
CHUNKS = len(CHUNK_HEADS)
STARTS = tuple(sum(CHUNK_HEADS[:c]) * HEAD_DIM for c in range(CHUNKS))
WIDTHS = tuple(n * HEAD_DIM for n in CHUNK_HEADS)
AHEAD = 3
SIDES_AHEAD = 9
PARTNER_LAG = 1
ATTEND_LAG = 3
QUERY_TILE = 256
SLOTS = 3
MESH = pl.DeviceIdType.MESH


def side_entries(entries, low, high):
    found, rank = [], jnp.int32(0)
    for entry in entries:
        hit = (entry >= low) & (entry < high)
        found.append((hit, rank, entry - low))
        rank = rank + hit.astype(jnp.int32)
    return found


def slot_rows(found, slots):
    return [
        sum(jnp.where(hit & (rank == slot), place, 0) for hit, rank, place in found)
        for slot in range(slots)
    ]


def line_place(entry, member, distant):
    hop = lax.div(entry, distant) + 1
    source = lax.rem(member + hop, DILATION_TILES)
    place = lax.div(source, 2) * distant + lax.rem(entry, distant)
    return place, lax.rem(hop, 2) == 1


def kernel(cols, blocks, cycle, dilated, q_hbm, km_hbm, ke_hbm, vm_hbm, ve_hbm, out_hbm, *scratch):
    kv = scratch[0:CHUNKS]
    zbuf = scratch[CHUNKS : 2 * CHUNKS]
    pbuf = scratch[2 * CHUNKS : 3 * CHUNKS]
    cbuf = scratch[3 * CHUNKS : 4 * CHUNKS]
    psend = scratch[4 * CHUNKS : 5 * CHUNKS]
    csend = scratch[5 * CHUNKS : 6 * CHUNKS]
    (out_ref, out_sem, q_ref, km_ref, ke_ref, vm_ref, ve_ref, in_sem, asked, heard, heard_s, req_send, req_recv, req_local, z_send, z_recv, f_send, p_send, p_recv,
     c_send, c_recv, e_send, e_recv, v_send, v_recv) = scratch[6 * CHUNKS :]
    block = kv[0].shape[-2]
    groups = ke_ref.shape[1]
    distant = blocks // 4
    spacing = cols // DILATION_TILES

    def fetch(src, dst, k):
        return pltpu.make_async_copy(src, dst, in_sem.at[k])

    pairs = ((km_hbm, km_ref), (vm_hbm, vm_ref))
    exponents = [fetch(ke_hbm, ke_ref, 0), fetch(ve_hbm, ve_ref, 1)]
    near = [
        fetch(src.at[4 * r], dst.at[4 * r], 2 + 2 * r + k)
        for r in range(distant) for k, (src, dst) in enumerate(pairs)
    ]
    far = [
        fetch(src.at[pl.ds(4 * r + 1, 3)], dst.at[pl.ds(4 * r + 1, 3)], 2 + 2 * (distant + r) + k)
        for r in range(distant) for k, (src, dst) in enumerate(pairs)
    ]
    queries = fetch(q_hbm, q_ref, 2 + 4 * distant)
    for part in (*exponents, *near, *far, queries):
        part.start()

    col = lax.axis_index("col")
    row = lax.axis_index("row")
    member, offset = col // spacing, lax.rem(col, spacing)
    gz, gy = member // 2, lax.rem(member, 2)

    def on_line(z):
        return {"col": (z * 2 + gy) * spacing + offset}

    partner = {"col": (gz * 2 + 1 - gy) * spacing + offset}
    left, right = {"col": col - 1}, {"col": col + 1}
    other = {"row": 1 - row}
    has_left, has_right = col > 0, col < cols - 1

    barrier = pltpu.get_barrier_semaphore()

    def greet(device):
        pl.semaphore_signal(barrier, inc=1, device_id=device, device_id_type=MESH)

    for z in range(LINE):
        pl.when(gz != z)(functools.partial(greet, on_line(z)))
    greet(partner)
    greet(other)
    pl.when(has_left)(functools.partial(greet, left))
    pl.when(has_right)(functools.partial(greet, right))

    def dequant(b):
        for which, (mant, expo) in enumerate(((km_ref, ke_ref), (vm_ref, ve_ref))):
            factor = lax.shift_left(jnp.int32(1), expo[b] + 8).astype(jnp.float32) * (2.0**-8)
            size = block // groups
            parts = [
                mant[b, g * size : (g + 1) * size, :].astype(jnp.float32) * factor[g : g + 1, :]
                for g in range(groups)
            ]
            full = jnp.concatenate(parts, axis=0).astype(jnp.bfloat16)
            for c in range(CHUNKS):
                kv[c][b, which] = full[:, STARTS[c] : STARTS[c] + WIDTHS[c]]

    lane = lax.broadcasted_iota(jnp.int32, asked.shape, 1)
    numbers = [cycle[i] for i in range(4)] + [dilated[i] for i in range(4)]
    asked[...] = sum(jnp.where(lane == i, number, 0) for i, number in enumerate(numbers))
    for part in (*exponents, *near):
        part.wait()
    for r in range(distant):
        dequant(4 * r)
        for c in range(CHUNKS):
            zbuf[c][gz * distant + r] = kv[c][4 * r]

    pl.semaphore_wait(barrier, LINE + 1 + has_left.astype(jnp.int32) + has_right.astype(jnp.int32))

    def copy(src, dst, send, recv, device):
        return pltpu.make_async_remote_copy(
            src_ref=src, dst_ref=dst, send_sem=send, recv_sem=recv,
            device_id=device, device_id_type=MESH,
        )

    def ask(k, device):
        return copy(asked, heard.at[k], req_send.at[k], req_recv.at[k], device)

    ask(0, partner).start()
    pl.when(has_left)(lambda: ask(2, left).start())
    pl.when(has_right)(lambda: ask(1, right).start())

    def line_copy(c, source, z, sem):
        part = zbuf[c].at[pl.ds(source * distant, distant)]
        return copy(part, part, sem, z_recv.at[c, source], on_line(z))

    steps = (2, -2, 1, -1)

    def reaches(step):
        return (gz + step >= 0) & (gz + step < LINE)

    def send_line(c):
        for k, step in enumerate(steps):
            pl.when(reaches(step))(
                lambda k=k, step=step: line_copy(c, gz, gz + step, z_send.at[c, k]).start()
            )

    for c in range(AHEAD):
        send_line(c)
    for part in far:
        part.wait()
    for b in range(blocks):
        if b % 4:
            dequant(b)

    def vertical(c):
        src = kv[c].at[(1 - row) * (blocks - 1)]
        return copy(src, cbuf[c].at[2 * SLOTS], v_send.at[c], v_recv.at[c], other)

    def local(k):
        return pltpu.make_async_copy(heard.at[k], heard_s.at[k], req_local.at[k])

    def listen(k, device):
        ask(k, device).wait_recv()
        local(k).start()
        local(k).wait()

    listen(0, partner)
    pl.when(has_left)(lambda: listen(1, left))
    pl.when(has_right)(lambda: listen(2, right))

    def side_copy(c, side, device):
        base = SLOTS * (1 - side)
        return copy(
            csend[c].at[pl.ds(side * SLOTS, 2)], cbuf[c].at[pl.ds(base, 2)],
            c_send.at[c, side], c_recv.at[c, 1 - side], device,
        )

    def edge_copy(c, side, device):
        base = SLOTS * (1 - side)
        return copy(
            csend[c].at[side * SLOTS + 2], cbuf[c].at[base + 2],
            e_send.at[c, side], e_recv.at[c, 1 - side], device,
        )

    sides = ((0, has_left, col == 1, left), (1, has_right, col == cols - 2, right))

    def send_sides(c):
        vertical(c).start()
        for side, exists, edge, device in sides:
            low = 2 + blocks * (1 - side)

            @pl.when(exists)
            def _():
                entries = [heard_s[1 + side, 0, i] for i in range(4)]
                rows = slot_rows(side_entries(entries, low, low + blocks), SLOTS)
                for j in range(2):
                    csend[c][side * SLOTS + j] = kv[c][rows[j]]
                side_copy(c, side, device).start()

                @pl.when(edge)
                def _():
                    csend[c][side * SLOTS + 2] = kv[c][rows[2]]
                    edge_copy(c, side, device).start()

    def forward(c):
        @pl.when(gz == 1)
        def _():
            line_copy(c, 3, 1, z_send.at[c, 0]).wait_recv()
            line_copy(c, 3, 0, f_send.at[c]).start()

        @pl.when(gz == 2)
        def _():
            line_copy(c, 0, 2, z_send.at[c, 0]).wait_recv()
            line_copy(c, 0, 3, f_send.at[c]).start()

    def partner_copy(c):
        return copy(psend[c], pbuf[c], p_send.at[c], p_recv.at[c], partner)

    def send_partner(c):
        for source in range(LINE):
            taken = ((gz == 1) & (source == 3)) | ((gz == 2) & (source == 0))
            pl.when((gz != source) & jnp.logical_not(taken))(
                lambda: line_copy(c, source, gz, z_send.at[c, 0]).wait_recv()
            )
        for i in range(4):
            place, _ = line_place(heard_s[0, 0, 4 + i], gz * 2 + 1 - gy, distant)
            psend[c][i] = zbuf[c][place]
        partner_copy(c).start()

    def wait_inputs(c):
        partner_copy(c).wait_recv()
        vertical(c).wait_recv()
        pl.when(has_left)(lambda: side_copy(c, 1, left).wait_recv())
        pl.when(has_right)(lambda: side_copy(c, 0, right).wait_recv())
        pl.when(col == cols - 1)(lambda: edge_copy(c, 1, left).wait_recv())
        pl.when(col == 0)(lambda: edge_copy(c, 0, right).wait_recv())

    entries = [cycle[i] for i in range(4)]
    lefts = side_entries(entries, 2, 2 + blocks)
    rights = side_entries(entries, 2 + blocks, 2 + 2 * blocks)
    cycle_places = [
        jnp.where(a[0], a[1], jnp.where(b[0], SLOTS + b[1], 2 * SLOTS))
        for a, b in zip(lefts, rights)
    ]

    def deliver(c):
        lanes = pl.ds(STARTS[c], WIDTHS[c])
        return pltpu.make_async_copy(out_ref.at[:, lanes], out_hbm.at[:, lanes], out_sem.at[c])

    def attend(c):
        for i in range(4):
            kv[c][blocks + i] = cbuf[c][cycle_places[i]]
            place, crossing = line_place(dilated[i], member, distant)
            kv[c][blocks + 4 + i] = jnp.where(crossing, pbuf[c][i], zbuf[c][place])
        factor = HEAD_DIM**-0.5 * math.log2(math.e)

        def tile(t, carry):
            rows = pl.ds(pl.multiple_of(t * QUERY_TILE, QUERY_TILE), QUERY_TILE)
            for h in range(CHUNK_HEADS[c]):
                lanes = slice(h * HEAD_DIM, (h + 1) * HEAD_DIM)
                whole = slice(STARTS[c] + h * HEAD_DIM, STARTS[c] + (h + 1) * HEAD_DIM)
                keys = kv[c][:, 0, :, lanes].reshape(-1, HEAD_DIM)
                values = kv[c][:, 1, :, lanes].reshape(-1, HEAD_DIM)
                dots = lax.dot_general(
                    q_ref[rows, whole], keys, (((1,), (1,)), ((), ())),
                    preferred_element_type=jnp.float32,
                )
                top = jnp.max(dots, axis=-1, keepdims=True)
                weights = jnp.exp2((dots - top) * factor)
                total = jnp.sum(weights, axis=-1, keepdims=True)
                blended = jnp.dot(
                    weights.astype(jnp.bfloat16), values, preferred_element_type=jnp.float32
                )
                out_ref[rows, whole] = (blended / total).astype(jnp.bfloat16)
            return carry

        lax.fori_loop(0, q_ref.shape[0] // QUERY_TILE, tile, 0)
        deliver(c).start()

    for c in range(SIDES_AHEAD):
        send_sides(c)
    queries.wait()
    for t in range(CHUNKS + ATTEND_LAG):
        if t < CHUNKS:
            forward(t)
        if t + AHEAD < CHUNKS:
            send_line(t + AHEAD)
        if t + SIDES_AHEAD < CHUNKS:
            send_sides(t + SIDES_AHEAD)
        if 0 <= t - PARTNER_LAG < CHUNKS:
            send_partner(t - PARTNER_LAG)
        if t >= ATTEND_LAG:
            wait_inputs(t - ATTEND_LAG)
            attend(t - ATTEND_LAG)

    ask(0, partner).wait_send()
    pl.when(has_left)(lambda: ask(2, left).wait_send())
    pl.when(has_right)(lambda: ask(1, right).wait_send())
    for c in range(CHUNKS):
        for k, step in enumerate(steps):
            pl.when(reaches(step))(
                lambda c=c, k=k, step=step: line_copy(c, gz, gz, z_send.at[c, k]).wait_send()
            )
        pl.when((gz == 1) | (gz == 2))(lambda: line_copy(c, 0, 0, f_send.at[c]).wait_send())
        deliver(c).wait()
        partner_copy(c).wait_send()
        vertical(c).wait_send()
        pl.when(has_left)(lambda: side_copy(c, 0, left).wait_send())
        pl.when(has_right)(lambda: side_copy(c, 1, right).wait_send())
        pl.when(col == 1)(lambda: edge_copy(c, 0, left).wait_send())
        pl.when(col == cols - 2)(lambda: edge_copy(c, 1, right).wait_send())


def per_device(queries, key_mant, key_exp, value_mant, value_exp, cycle_list, dilated_list):
    blocks, _, block, features = queries.shape
    groups = key_exp.shape[2]
    cols = lax.axis_size("col")
    distant = blocks // 4
    vmem = pltpu.VMEM
    smem = pl.BlockSpec(memory_space=pltpu.SMEM)
    anywhere = pl.BlockSpec(memory_space=pl.ANY)

    def buffers(slots):
        return [vmem((slots, 2, block, width), jnp.bfloat16) for width in WIDTHS]

    dma = pltpu.SemaphoreType.DMA
    tokens = blocks * block
    out = pl.pallas_call(
        functools.partial(kernel, cols, blocks),
        out_shape=jax.ShapeDtypeStruct((tokens, features), jnp.bfloat16),
        in_specs=[smem] * 2 + [anywhere] * 5,
        out_specs=anywhere,
        scratch_shapes=[
            *buffers(blocks + 8), *buffers(LINE * distant), *buffers(4),
            *buffers(2 * SLOTS + 1), *buffers(4), *buffers(2 * SLOTS),
            vmem((tokens, features), jnp.bfloat16), dma((CHUNKS,)),
            vmem((tokens, features), jnp.bfloat16),
            *[
                part
                for _ in range(2)
                for part in (
                    vmem((blocks, block, features), jnp.bfloat16),
                    vmem((blocks, groups, features), jnp.int32),
                )
            ],
            dma((3 + 4 * distant,)), vmem((8, 128), jnp.int32),
            pltpu.VMEM((3, 8, 128), jnp.int32), pltpu.SMEM((3, 8, 128), jnp.int32),
            dma((3,)), dma((3,)), dma((3,)),
            dma((CHUNKS, 4)), dma((CHUNKS, LINE)), dma((CHUNKS,)),
            dma((CHUNKS,)), dma((CHUNKS,)),
            dma((CHUNKS, 2)), dma((CHUNKS, 2)), dma((CHUNKS, 2)), dma((CHUNKS, 2)),
            dma((CHUNKS,)), dma((CHUNKS,)),
        ],
        compiler_params=pltpu.CompilerParams(
            collective_id=0, has_side_effects=True, vmem_limit_bytes=60 * 2**20
        ),
        cost_estimate=pl.CostEstimate(
            flops=8 * tokens * tokens * features, bytes_accessed=10 * tokens * features,
            transcendentals=2 * tokens * tokens * HEADS,
        ),
    )(
        cycle_list.reshape(-1), dilated_list.reshape(-1), queries.reshape(tokens, features),
        key_mant.reshape(blocks, block, features), key_exp.reshape(blocks, groups, features),
        value_mant.reshape(blocks, block, features), value_exp.reshape(blocks, groups, features),
    )
    return out.reshape(queries.shape)


def solution(mesh):
    split = P(("groups", "row"), "col", None, None)
    lists = P(("groups", "row"), "col", None)
    return jax.shard_map(
        per_device, mesh=mesh, in_specs=(split,) * 5 + (lists,) * 2, out_specs=split,
        check_vma=False,
    )
```
